32 devices in a mesh: dp: 4 (over z), row: 4 (over y, core), col: 2 (over x).
Axes of the slice: x: 2, y: 2, z: 4, core: 2. Of those that a mesh axis runs over, the one named last changes fastest.
Arguments:
- inputs: bfloat16 [8192, 2048], P(('dp', 'row'), 'col'), may hold values from -6 to 6
- segments: int32 [8, 1024], P('dp'), may hold values from 0 to 6, as said below
- norm1_gain: bfloat16 [2048], P('col'), may hold values from 0.25 to 1.75
- query_weight: bfloat16 [2048, 2048], P('col', 'row'), may hold values from -0.125 to 0.125
- key_weight: bfloat16 [2048, 256], P('col', 'row'), may hold values from -0.125 to 0.125
- value_weight: bfloat16 [2048, 256], P('col', 'row'), may hold values from -0.125 to 0.125
- out_weight: bfloat16 [2048, 2048], P('row', 'col'), may hold values from -0.5 to 0.5
- norm2_gain: bfloat16 [2048], P('col'), may hold values from 0.25 to 1.75
- gate_weight: bfloat16 [2048, 5632], P('col', 'row'), may hold values from -0.125 to 0.125
- up_weight: bfloat16 [2048, 5632], P('col', 'row'), may hold values from -0.125 to 0.125
- down_weight: bfloat16 [5632, 2048], P('row', 'col'), may hold values from -0.109375 to 0.109375
- cotangent: bfloat16 [8192, 2048], P(('dp', 'row'), 'col'), may hold values from -6 to 6
Outputs:
- outputs: bfloat16 [8192, 2048], P(('dp', 'row'), 'col')
- grad_inputs: float32 [8192, 2048], P(('dp', 'row'), 'col')
- grad_norm1: float32 [2048], P('col')
- grad_query: float32 [2048, 2048], P('col', 'row')
- grad_key: float32 [2048, 256], P('col', 'row')
- grad_value: float32 [2048, 256], P('col', 'row')
- grad_out: float32 [2048, 2048], P('row', 'col')
- grad_norm2: float32 [2048], P('col')
- grad_gate: float32 [2048, 5632], P('col', 'row')
- grad_up: float32 [2048, 5632], P('col', 'row')
- grad_down: float32 [5632, 2048], P('row', 'col')
The draws below stay inside these ranges and needn't reach their ends.
Inputs may be any that keep to these rules, and one draw needn't show every extreme that they name: `segments`: within each sequence the numbers start at 0 and rise by 0 or 1 from one token to the next; equal numbers mark one document.
All inputs are finite; a program needn't handle non-finite values.
Results may differ from the reference program's by a relative error of at most 0.018.
Values may be sent and summed in bfloat16 or wider, within the bound.
No kernel may reach another device: no remote copies, remote signals or barrier semaphores. Data moves between devices by JAX's collectives and lax.ppermute only.
A program may use at most 320 MiB of HBM per device.

```python
import jax
import jax.numpy as jnp
from jax import lax

D = 2048
HQ = 32
KV = 4
HD = 64
FF = 5632
LEN = 1024
SEQ_DP = 2
SEQS = 8
TOKENS = 8192


def draw_segments(key, part):
    key = jax.random.fold_in(key, 11)
    key_length, key_offset, key_pick = jax.random.split(key, 3)
    shortest = max(LEN * 200 // 1024, 2)
    longest = LEN * 2000 // 1024
    lengths = jax.random.randint(key_length, (SEQS, LEN), shortest, longest + 1)
    offset = jax.random.randint(key_offset, (SEQS, 1), 0, 1 << 20) % lengths[:, :1]
    ends = jnp.cumsum(lengths, 1) - offset
    indices = jnp.arange(LEN, dtype=jnp.int32)
    numbers = jax.vmap(lambda row_ends: jnp.searchsorted(row_ends, indices, side='right'))(ends).astype(jnp.int32)
    chosen = jax.random.randint(key_pick, (SEQS // SEQ_DP, 1), 0, SEQ_DP)
    within = jnp.arange(SEQS, dtype=jnp.int32).reshape(SEQS // SEQ_DP, SEQ_DP) % SEQ_DP
    single = (within == chosen).reshape(SEQS)
    densest = jnp.where(indices == 0, 0, (indices - 1) // shortest + 1).astype(jnp.int32)
    packed_most = jnp.arange(SEQS, dtype=jnp.int32) == (chosen[0, 0] + 1) % SEQ_DP
    numbers = jnp.where(packed_most[:, None], densest[None, :], numbers)
    return jnp.where(single[:, None], 0, numbers).astype(jnp.int32)


def levels(stream_key, dims, shards, smallest, largest):
    loudness = 1.0
    for position, parts in shards:
        steps = jax.random.uniform(jax.random.fold_in(jax.random.fold_in(stream_key, 6), position), (parts,), jnp.float32, smallest / len(shards), largest / len(shards))
        loudness = loudness * jnp.repeat(jnp.exp(steps), dims[position] // parts).reshape((-1,) + (1,) * (len(dims) - 1 - position))
    return loudness


def normal_values(stream_key, dims, spread, reach, cuts=(), kind=jnp.bfloat16):
    array = jax.random.normal(stream_key, dims, jnp.float32) * spread
    if len(cuts) > 0:
        array = levels(stream_key, dims, cuts, -0.22, 0.18) * array
    return jnp.clip(array, min=-reach, max=reach).astype(kind)


def setup_inputs(seed: int = 0) -> dict:
    key_of = jax.random.split(jax.random.key(seed), 13)
    inputs = normal_values(key_of[0], (TOKENS, D), 1.0, 6.0, ((0, 16), (1, 2)))
    segments = draw_segments(jax.random.fold_in(key_of[12], 71), 0)
    norm1_gain = jnp.clip(1.0 + 0.15 * jax.random.normal(key_of[2], (D,), jnp.float32), 0.25, 1.75).astype(jnp.bfloat16)
    query_weight = normal_values(key_of[3], (D, HQ * HD), D ** -0.5, 0.125, ((0, 2), (1, 4)))
    key_weight = normal_values(key_of[4], (D, KV * HD), D ** -0.5, 0.125, ((0, 2), (1, 4)))
    value_weight = normal_values(key_of[5], (D, KV * HD), D ** -0.5, 0.125, ((0, 2), (1, 4)))
    out_weight = normal_values(key_of[6], (HQ * HD, D), (HQ * HD // 16) ** -0.5, 0.5, ((0, 4), (1, 2)))
    norm2_gain = jnp.clip(1.0 + 0.15 * jax.random.normal(key_of[7], (D,), jnp.float32), 0.25, 1.75).astype(jnp.bfloat16)
    gate_weight = normal_values(key_of[8], (D, FF), D ** -0.5, 0.125, ((0, 2), (1, 4)))
    up_weight = normal_values(key_of[9], (D, FF), D ** -0.5, 0.125, ((0, 2), (1, 4)))
    down_weight = normal_values(key_of[10], (FF, D), (FF // 2) ** -0.5, 0.109375, ((0, 4), (1, 2)))
    cotangent = normal_values(key_of[11], (TOKENS, D), 1.0, 6.0, ((0, 16), (1, 2)))
    return {"inputs": inputs, "segments": segments, "norm1_gain": norm1_gain, "query_weight": query_weight, "key_weight": key_weight, "value_weight": value_weight, "out_weight": out_weight, "norm2_gain": norm2_gain, "gate_weight": gate_weight, "up_weight": up_weight, "down_weight": down_weight, "cotangent": cotangent}


epsilon = 1e-05
rope_base = 10000.0

@jax.custom_vjp
def low(v):
    return lax.optimization_barrier(v.astype(jnp.bfloat16)).astype(jnp.float32)

@jax.custom_vjp
def low_back(v):
    return v

def low_keep(v):
    return (low(v), None)

def low_pass(kept, grad):
    return (grad,)

def back_keep(v):
    return (v, None)

def back_low(kept, grad):
    return (low(grad),)
low.defvjp(low_keep, low_pass)
low_back.defvjp(back_keep, back_low)

def highest(leading, trailing):
    return jnp.dot(leading, trailing, precision=lax.Precision.HIGHEST, preferred_element_type=jnp.float32)

def positions_of(segment_row):
    indices = jnp.arange(segment_row.shape[0], dtype=jnp.int32)
    previous = jnp.concatenate([segment_row[:1] - 1, segment_row[:-1]])
    start_index = lax.cummax(jnp.where(segment_row != previous, indices, 0), axis=0)
    return indices - start_index

def rotate(vectors, positions):
    half_width = vectors.shape[-1] // 2
    frequency = rope_base ** (-jnp.arange(half_width).astype(jnp.float32) * 2.0 / vectors.shape[-1])
    angles = positions.astype(jnp.float32)[..., None] * frequency
    cosine = jnp.concatenate([jnp.cos(angles), jnp.cos(angles)], -1)[..., None, :]
    sine_table = jnp.concatenate([jnp.sin(angles), jnp.sin(angles)], -1)[..., None, :]
    turned = jnp.concatenate([-vectors[..., half_width:], vectors[..., :half_width]], -1)
    return vectors * cosine + turned * sine_table

def attend_sequence(packed):
    queries, key_rows, value_rows, segment_row = packed
    length, query_heads, head_dim = queries.shape
    pair_heads = key_rows.shape[1]
    grouped = queries.reshape(length, pair_heads, query_heads // pair_heads, head_dim)
    scores = jnp.einsum('qkgd,skd->kgqs', grouped, key_rows, precision=lax.Precision.HIGHEST) * head_dim ** (-0.5)
    scores = low_back(scores)
    indices = jnp.arange(length, dtype=jnp.int32)
    allowed = (segment_row[:, None] == segment_row[None, :]) & (indices[:, None] >= indices[None, :])
    scores = jnp.where(allowed, scores, -1e+30)
    highest_score = lax.optimization_barrier(jnp.max(scores, -1, keepdims=True))
    weights = jnp.exp(scores - highest_score)
    weights = low(weights / lax.optimization_barrier(jnp.sum(weights, -1, keepdims=True)))
    mixture = jnp.einsum('kgqs,skd->qkgd', weights, value_rows, precision=lax.Precision.HIGHEST)
    return mixture.reshape(length, query_heads * head_dim)

def rms_normed(values):
    return values * lax.rsqrt(lax.optimization_barrier(jnp.mean(values * values, -1, keepdims=True)) + epsilon)

def layer(features, seg_rows, gain_one, query_weight, key_weight, value_weight, out_weight, gain_two, gate_weight, up_weight, down_weight):
    sequence_count = seg_rows.shape[0]
    length = seg_rows.shape[1]
    query_width = query_weight.shape[1]
    pair_width = key_weight.shape[1]
    hidden_one = low(rms_normed(features) * gain_one)
    joined = low_back(highest(hidden_one, jnp.concatenate([query_weight, key_weight, value_weight], 1)))
    positions = jax.vmap(positions_of)(seg_rows)
    queries = low(rotate(joined[:, :query_width].reshape(sequence_count, length, -1, HD), positions))
    key_rows = low(rotate(joined[:, query_width:query_width + pair_width].reshape(sequence_count, length, -1, HD), positions))
    value_rows = low(joined[:, query_width + pair_width:].reshape(sequence_count, length, -1, HD))
    attended = lax.map(jax.checkpoint(attend_sequence), (queries, key_rows, value_rows, seg_rows))
    attended = low(low_back(attended.reshape(sequence_count * length, query_width)))
    middle = features + low_back(highest(attended, out_weight))
    hidden_two = low(rms_normed(middle) * gain_two)
    gate_part = low_back(highest(hidden_two, gate_weight))
    up_part = low_back(highest(hidden_two, up_weight))
    activated = low(jax.nn.silu(gate_part) * up_part)
    return middle + low_back(highest(activated, down_weight))

def reference(inputs, segments, norm1_gain, query_weight, key_weight, value_weight, out_weight, norm2_gain, gate_weight, up_weight, down_weight, cotangent):
    params = tuple((tensor.astype(jnp.float32) for tensor in (norm1_gain, query_weight, key_weight, value_weight, out_weight, norm2_gain, gate_weight, up_weight, down_weight)))
    groups = segments.shape[0] // SEQ_DP
    block_rows = SEQ_DP * LEN
    features = inputs.astype(jnp.float32).reshape(groups, block_rows, D)
    cotangents = cotangent.astype(jnp.float32).reshape(groups, block_rows, D)
    seg_blocks = segments.reshape(groups, SEQ_DP, LEN)

    def accumulate(running, packed):
        block_in, block_seg, block_cot = packed

        def apply_layer(block, *weights):
            return layer(block, block_seg, *weights)
        result, pullback = jax.vjp(apply_layer, block_in, *params)
        gradients = pullback(block_cot)
        running = tuple((before + addend for before, addend in zip(running, gradients[1:])))
        return (running, (result.astype(jnp.bfloat16), gradients[0]))
    initial = tuple((jnp.zeros(tensor.shape, jnp.float32) for tensor in params))
    running, (results, grad_inputs) = lax.scan(accumulate, initial, (features, seg_blocks, cotangents))
    return (results.reshape(-1, D), grad_inputs.reshape(-1, D), running[0], running[1], running[2], running[3], running[4], running[5], running[6], running[7], running[8])
```

```python
import jax
import jax.numpy as jnp
from jax import lax
from jax.sharding import PartitionSpec as P

HD = 64
LANES = 128

epsilon = 1e-05
rope_base = 10000.0
BF = jnp.bfloat16
F32 = jnp.float32


def positions_of(segment_row):
    indices = jnp.arange(segment_row.shape[0], dtype=jnp.int32)
    previous = jnp.concatenate([segment_row[:1] - 1, segment_row[:-1]])
    start_index = lax.cummax(jnp.where(segment_row != previous, indices, 0), axis=0)
    return indices - start_index


def rotary_tables(positions):
    half_width = HD // 2
    frequency = rope_base ** (-jnp.arange(half_width).astype(F32) * 2.0 / HD)
    angles = positions.astype(F32)[..., None] * frequency
    cosine = jnp.concatenate([jnp.cos(angles), jnp.cos(angles)], -1)
    sine = jnp.concatenate([jnp.sin(angles), jnp.sin(angles)], -1)
    return cosine, sine


def rotate(vectors, cosine, sine):
    half_width = HD // 2
    turned = jnp.concatenate([-vectors[..., half_width:], vectors[..., :half_width]], -1)
    return vectors * cosine[:, None, :] + turned * sine[:, None, :]


def swap(values, axis, bit):
    pairs = [(i, i ^ bit) for i in range(lax.axis_size(axis))]
    return lax.ppermute(values, axis, pairs)


def swap_sum(values):
    return values + swap(values, "col", 1)


def pick(values, index, axis):
    return lax.dynamic_index_in_dim(values, index, axis, keepdims=False)


def pair_up(own, other, first, axis):
    return jnp.concatenate([jnp.where(first, own, other), jnp.where(first, other, own)], axis)


def gather_row(block):
    size = lax.axis_size("row")
    blocks = {0: block}
    bit = size // 2
    while bit:
        for offset in list(blocks):
            blocks[offset | bit] = swap(blocks[offset], "row", bit)
        bit //= 2
    me = lax.axis_index("row")
    whole = jnp.zeros((size * block.shape[0],) + block.shape[1:], block.dtype)
    for offset, part in blocks.items():
        whole = lax.dynamic_update_slice_in_dim(whole, part, (me ^ offset) * block.shape[0], 0)
    return whole


def scatter_row(partial):
    size = lax.axis_size("row")
    me = lax.axis_index("row")
    current = partial
    while size > 1:
        block = partial.shape[0] // lax.axis_size("row")
        current = current.reshape(size // 2, 2, block, partial.shape[1])
        kept = pick(current, me & 1, 1).astype(F32)
        sent = pick(current, 1 - (me & 1), 1).astype(BF)
        bit = lax.axis_size("row") // size
        current = kept + swap(sent, "row", bit).astype(F32)
        me = me >> 1
        size //= 2
    return current.reshape(partial.shape[0] // lax.axis_size("row"), partial.shape[1])


def gather_plane(block):
    half = block.shape[0] // 2
    across = swap(block, "col", 1)
    along = swap(block, "row", 2)
    corner = jnp.concatenate([swap(along[:half], "col", 1), swap(across[half:], "row", 2)], 0)
    near = jnp.concatenate([block, across], 1)
    far = jnp.concatenate([along, corner], 1)
    near_sibling = jnp.concatenate([swap(block, "row", 1), swap(across, "row", 1)], 1)
    far_sibling = jnp.concatenate([swap(along, "row", 1), swap(corner, "row", 1)], 1)
    return jnp.concatenate([near, near_sibling, far, far_sibling], 0)


def scatter_plane(partial):
    rows = partial.shape[0] // 4
    width = partial.shape[1] // 2
    half = rows // 2
    blocks = partial.reshape(2, 2, rows, 2 * width)
    summed = blocks[:, 0].astype(F32) + swap(blocks[:, 1].astype(BF), "row", 1).astype(F32)
    first = summed[:, :half]
    second = summed[:, half:]
    first_sum = first[:, :, :width] + swap(first[:, :, width:].astype(BF), "col", 1).astype(F32)
    first_sum = first_sum[0] + swap(first_sum[1].astype(BF), "row", 2).astype(F32)
    second_sum = second[0] + swap(second[1].astype(BF), "row", 2).astype(F32)
    second_sum = second_sum[:, :width] + swap(second_sum[:, width:].astype(BF), "col", 1).astype(F32)
    return jnp.concatenate([first_sum, second_sum], 0)


def sum_dp(values):
    size = lax.axis_size("dp")
    if size != 4:
        mine = lax.psum_scatter(values, "dp", scatter_dimension=0, tiled=True)
        return lax.all_gather(mine, "dp", axis=0, tiled=True)
    place = lax.axis_index("dp")
    inward = lax.ppermute(values, "dp", [(0, 1), (3, 2)])
    half_sum = (values.astype(F32) + inward.astype(F32)).astype(BF)
    crossed = lax.ppermute(half_sum, "dp", [(1, 2), (2, 1)])
    total = (half_sum.astype(F32) + crossed.astype(F32)).astype(BF)
    outward = lax.ppermute(total, "dp", [(1, 0), (2, 3)])
    return jnp.where((place == 0) | (place == 3), outward, total)


def norm_forward(values, gain, full_width):
    squares = swap_sum(jnp.sum(values * values, -1, keepdims=True))
    scale = lax.rsqrt(squares / full_width + epsilon)
    normed = values * scale
    return (normed, scale, (normed * gain).astype(BF))


def norm_backward(grad_hidden, normed, scale, gain, full_width):
    grad_normed = grad_hidden * gain
    inner_sum = swap_sum(jnp.sum(grad_normed * normed, -1, keepdims=True))
    return (
        scale * (grad_normed - normed * inner_sum / full_width),
        jnp.sum(grad_hidden * normed, 0),
    )


def contract(leading, weight, kind=F32):
    return jnp.dot(leading, weight, preferred_element_type=F32).astype(kind)


def contract_flipped(leading, weight, kind=F32):
    return lax.dot_general(
        leading, weight, (((1,), (1,)), ((), ())), preferred_element_type=F32
    ).astype(kind)


def outer_sum(leading, trailing):
    return lax.dot_general(
        leading, trailing, (((0,), (0,)), ((), ())), preferred_element_type=F32
    ).astype(BF)


def score_block(queries, key_rows, segment_row):
    length = queries.shape[0]
    pair_heads = key_rows.shape[1] // HD
    grouped = queries.reshape(length, pair_heads, -1, HD)
    keyed = key_rows.reshape(length, pair_heads, HD)
    scores = jnp.einsum("qkgd,skd->kgqs", grouped, keyed, preferred_element_type=F32) * HD ** (-0.5)
    indices = jnp.arange(length, dtype=jnp.int32)
    allowed = (segment_row[:, None] == segment_row[None, :]) & (
        indices[:, None] >= indices[None, :]
    )
    return (grouped, keyed, jnp.where(allowed, scores, -1e30), allowed)


def attention_forward(packed):
    queries, key_rows, value_rows, segment_row = packed
    grouped, keyed, scores, allowed = score_block(queries, key_rows, segment_row)
    highest_score = jnp.max(scores, -1, keepdims=True)
    weights = jnp.exp(scores - highest_score)
    totals = jnp.sum(weights, -1, keepdims=True)
    weights_low = (weights / totals).astype(BF)
    valued = value_rows.reshape(keyed.shape)
    mixture = jnp.einsum("kgqs,skd->qkgd", weights_low, valued, preferred_element_type=F32)
    return (mixture.reshape(queries.shape).astype(BF), highest_score + jnp.log(totals))


def attention_backward(packed):
    queries, key_rows, value_rows, segment_row, log_total, grad_mixture = packed
    grouped, keyed, scores, allowed = score_block(queries, key_rows, segment_row)
    weights = jnp.where(allowed, jnp.exp(scores - log_total), 0.0)
    valued = value_rows.reshape(keyed.shape)
    grad_grouped = grad_mixture.reshape(grouped.shape)
    grad_weights = jnp.einsum("qkgd,skd->kgqs", grad_grouped, valued, preferred_element_type=F32)
    row_inner = jnp.sum(weights * grad_weights, -1, keepdims=True)
    grad_scores = (weights * (grad_weights - row_inner)).astype(BF)
    scale_factor = HD ** (-0.5)
    grad_queries = (
        jnp.einsum("kgqs,skd->qkgd", grad_scores, keyed, preferred_element_type=F32) * scale_factor
    )
    grad_keys = (
        jnp.einsum("kgqs,qkgd->skd", grad_scores, grouped, preferred_element_type=F32)
        * scale_factor
    )
    grad_values = jnp.einsum(
        "kgqs,qkgd->skd", weights.astype(BF), grad_grouped, preferred_element_type=F32
    )
    return (grad_queries.reshape(queries.shape[0], -1, HD), grad_keys, grad_values)


def body(
    inputs,
    segments,
    norm1_gain,
    query_weight,
    key_weight,
    value_weight,
    out_weight,
    norm2_gain,
    gate_weight,
    up_weight,
    down_weight,
    cotangent,
):
    columns = lax.axis_size("col")
    full_width = norm1_gain.shape[0] * columns
    width = norm1_gain.shape[0]
    query_width = query_weight.shape[1]
    pair_width = key_weight.shape[1]
    hidden_width = gate_weight.shape[1]
    per_column = segments.shape[0] // columns
    seq_length = segments.shape[1]
    column = lax.axis_index("col")
    first_column = column == 0

    part = -(-(hidden_width // 2) // LANES) * LANES
    overlap = 2 * part - hidden_width

    def cut(weight, axis):
        low = lax.slice_in_dim(weight, 0, part, axis=axis)
        high = lax.slice_in_dim(weight, hidden_width - part, hidden_width, axis=axis)
        inside = lax.broadcasted_iota(jnp.int32, high.shape, axis) >= overlap
        high = jnp.where(inside, high, jnp.zeros_like(high))
        kept = jnp.where(first_column, low, high)
        sent = jnp.where(first_column, high, low)
        return jnp.concatenate([kept, swap(sent, "col", 1)], 1 - axis)

    def uncut(grad, axis):
        own = lax.slice_in_dim(grad, 0, width, axis=1 - axis)
        other = swap(lax.slice_in_dim(grad, width, 2 * width, axis=1 - axis), "col", 1)
        low = jnp.where(first_column, own, other)
        high = lax.slice_in_dim(jnp.where(first_column, other, own), overlap, part, axis=axis)
        return jnp.concatenate([sum_dp(low), sum_dp(high)], axis).astype(F32)

    features = inputs.astype(F32)
    gain_one = norm1_gain.astype(F32)
    gain_two = norm2_gain.astype(F32)
    normed_one, scale_one, hidden_one = norm_forward(features, gain_one, full_width)
    hidden_one_all = gather_row(hidden_one)

    gate_full = cut(gate_weight, 1)
    up_full = cut(up_weight, 1)
    down_full = cut(down_weight, 0)
    cotangent_all = gather_plane(cotangent)

    qkv_weight = jnp.concatenate([query_weight, key_weight, value_weight], 1)
    local_segments = lax.dynamic_slice_in_dim(segments, column * per_column, per_column, 0)
    positions = jax.vmap(positions_of)(local_segments).reshape(-1)
    local_tokens = positions.shape[0]
    cosine, sine = rotary_tables(positions)

    def scatter_col(partial):
        split = partial.reshape(columns, local_tokens, partial.shape[1])
        return pick(split, column, 0) + swap(pick(split, 1 - column, 0).astype(BF), "col", 1).astype(F32)

    def gather_col(block):
        return pair_up(block, swap(block, "col", 1), first_column, 0)

    projected = scatter_col(contract(hidden_one_all, qkv_weight))
    queries = (
        rotate(projected[:, :query_width].reshape(local_tokens, -1, HD), cosine, sine)
        .reshape(local_tokens, query_width)
        .astype(BF)
    )
    key_rows = (
        rotate(
            projected[:, query_width : query_width + pair_width].reshape(local_tokens, -1, HD),
            cosine,
            sine,
        )
        .reshape(local_tokens, pair_width)
        .astype(BF)
    )
    value_rows = projected[:, query_width + pair_width :].astype(BF)
    by_sequence = (
        queries.reshape(per_column, seq_length, query_width),
        key_rows.reshape(per_column, seq_length, pair_width),
        value_rows.reshape(per_column, seq_length, pair_width),
        local_segments,
    )
    attended, log_totals = lax.map(attention_forward, by_sequence)
    attended_all = gather_col(attended.reshape(local_tokens, query_width))
    attn_branch = scatter_row(contract(attended_all, out_weight, BF))
    middle = features + attn_branch
    normed_two, scale_two, hidden_two = norm_forward(middle, gain_two, full_width)
    hidden_two_all = gather_plane(hidden_two)
    gate_part = contract(hidden_two_all, gate_full)
    up_part = contract(hidden_two_all, up_full)
    sigmoid_gate = jax.nn.sigmoid(gate_part)
    activated = (gate_part * sigmoid_gate * up_part).astype(BF)
    grad_activated = contract_flipped(cotangent_all, down_full)
    grad_gate_part = (
        grad_activated * up_part * sigmoid_gate * (1.0 + gate_part * (1.0 - sigmoid_gate))
    ).astype(BF)
    grad_up_part = (grad_activated * gate_part * sigmoid_gate).astype(BF)
    grad_hidden_two = scatter_plane(
        (
            contract_flipped(grad_gate_part, gate_full) + contract_flipped(grad_up_part, up_full)
        ).astype(BF)
    )
    outputs = (middle + scatter_plane(contract(activated, down_full, BF))).astype(BF)
    grad_down = uncut(outer_sum(activated, cotangent_all), 0)
    grad_gate = uncut(outer_sum(hidden_two_all, grad_gate_part), 1)
    grad_up = uncut(outer_sum(hidden_two_all, grad_up_part), 1)

    grad_norm_two, grad_gain_two = norm_backward(
        grad_hidden_two, normed_two, scale_two, gain_two, full_width
    )
    grad_middle = cotangent.astype(F32) + grad_norm_two
    branch_all = gather_row(grad_middle.astype(BF))
    grad_attended = scatter_col(contract_flipped(branch_all, out_weight)).astype(BF)
    grad_out = sum_dp(outer_sum(attended_all, branch_all)).astype(F32)
    grad_packed = by_sequence + (
        log_totals,
        grad_attended.reshape(per_column, seq_length, query_width),
    )
    grad_queries, grad_keys, grad_values = lax.map(attention_backward, grad_packed)
    grad_queries = rotate(grad_queries.reshape(local_tokens, -1, HD), cosine, -sine).reshape(
        local_tokens, query_width
    )
    grad_keys = rotate(grad_keys.reshape(local_tokens, -1, HD), cosine, -sine).reshape(
        local_tokens, pair_width
    )
    grad_projected = jnp.concatenate(
        [grad_queries, grad_keys, grad_values.reshape(local_tokens, pair_width)], 1
    ).astype(BF)
    projected_all = gather_col(grad_projected)
    grad_hidden_one = scatter_row(contract_flipped(projected_all, qkv_weight, BF))
    grad_qkv = sum_dp(outer_sum(hidden_one_all, projected_all)).astype(F32)
    grad_norm_one, grad_gain_one = norm_backward(
        grad_hidden_one, normed_one, scale_one, gain_one, full_width
    )
    grad_inputs = grad_middle + grad_norm_one
    gain_grads = lax.psum((grad_gain_one, grad_gain_two), ("dp", "row"))
    return (
        outputs,
        grad_inputs,
        gain_grads[0],
        grad_qkv[:, :query_width],
        grad_qkv[:, query_width : query_width + pair_width],
        grad_qkv[:, query_width + pair_width :],
        grad_out,
        gain_grads[1],
        grad_gate,
        grad_up,
        grad_down,
    )


def solution(mesh):
    in_specs = (
        P(("dp", "row"), "col"),
        P("dp", None),
        P("col"),
        P("col", "row"),
        P("col", "row"),
        P("col", "row"),
        P("row", "col"),
        P("col"),
        P("col", "row"),
        P("col", "row"),
        P("row", "col"),
        P(("dp", "row"), "col"),
    )
    out_specs = (
        P(("dp", "row"), "col"),
        P(("dp", "row"), "col"),
        P("col"),
        P("col", "row"),
        P("col", "row"),
        P("col", "row"),
        P("row", "col"),
        P("col"),
        P("col", "row"),
        P("col", "row"),
        P("row", "col"),
    )
    return jax.shard_map(body, mesh=mesh, in_specs=in_specs, out_specs=out_specs, check_vma=False)
```

```python
import jax
import jax.numpy as jnp
from jax import lax
from jax.experimental import pallas as pl
from jax.experimental.pallas import tpu as pltpu
from jax.sharding import PartitionSpec as P

HD = 64
LANES = 128

epsilon = 1e-05
rope_base = 10000.0
BF = jnp.bfloat16
F32 = jnp.float32


def positions_of(segment_row):
    indices = jnp.arange(segment_row.shape[0], dtype=jnp.int32)
    previous = jnp.concatenate([segment_row[:1] - 1, segment_row[:-1]])
    start_index = lax.cummax(jnp.where(segment_row != previous, indices, 0), axis=0)
    return indices - start_index


def rotary_tables(positions):
    frequency = rope_base ** (-jnp.arange(HD // 2).astype(F32) * 2.0 / HD)
    angles = positions.astype(F32)[..., None] * frequency
    cosine = jnp.cos(angles)
    sine = jnp.sin(angles)
    return (
        jnp.concatenate([cosine] * 4, -1),
        jnp.concatenate([-sine, sine, -sine, sine], -1),
    )


def swap(values, axis, bit):
    pairs = [(i, i ^ bit) for i in range(lax.axis_size(axis))]
    return lax.ppermute(values, axis, pairs)


def swap_sum(values):
    return values + swap(values, "col", 1)


def pick(values, index, axis):
    return lax.dynamic_index_in_dim(values, index, axis, keepdims=False)


def pair_up(own, other, first, axis):
    return jnp.concatenate([jnp.where(first, own, other), jnp.where(first, other, own)], axis)


def gather_row(block):
    size = lax.axis_size("row")
    blocks = {0: block}
    bit = size // 2
    while bit:
        for offset in list(blocks):
            blocks[offset | bit] = swap(blocks[offset], "row", bit)
        bit //= 2
    me = lax.axis_index("row")
    whole = jnp.zeros((size * block.shape[0],) + block.shape[1:], block.dtype)
    for offset, part in blocks.items():
        whole = lax.dynamic_update_slice_in_dim(whole, part, (me ^ offset) * block.shape[0], 0)
    return whole


def scatter_row(leading, product):
    me = lax.axis_index("row")
    block = leading.shape[0] // 4
    split = leading.reshape(2, 2, block, leading.shape[1])
    sent = product(pick(split, 1 - (me & 1), 1).reshape(2 * block, -1)).astype(BF)
    arrived = swap(sent, "row", 1)
    kept = product(pick(split, me & 1, 1).reshape(2 * block, -1))
    both = (kept + arrived.astype(F32)).reshape(2, block, -1)
    return pick(both, me >> 1, 0) + swap(
        pick(both, 1 - (me >> 1), 0).astype(BF), "row", 2
    ).astype(F32)


def gather_plane(block):
    half = block.shape[0] // 2
    across, along = yield (swap(block, "col", 1), swap(block, "row", 2))
    corner_first, corner_second = yield (
        swap(along[:half], "col", 1),
        swap(across[half:], "row", 2),
    )
    own = jnp.concatenate([block, along], 0)
    other = jnp.concatenate([across, corner_first, corner_second], 0)
    yield (
        jnp.concatenate([own, swap(own, "row", 1)], 0),
        jnp.concatenate([other, swap(other, "row", 1)], 0),
    )


def scatter_plane(kept, sent):
    arrived = [swap(values, "row", 1) for values in sent]
    own, other = [
        (values.astype(F32) + more.astype(F32)).reshape(2, -1, values.shape[1])
        for values, more in zip(kept, arrived)
    ]
    half = own.shape[1] // 2
    first_own, first_other = own[:, :half], other[:, :half].astype(BF)
    second_own, second_other = own[:, half:], other[:, half:]
    first_got = swap(first_other, "col", 1)
    second_got_own = swap(second_own[1].astype(BF), "row", 2)
    second_got_other = swap(second_other[1].astype(BF), "row", 2)
    first_got, second_got_own, second_got_other = yield (
        first_got,
        second_got_own,
        second_got_other,
    )
    first_sum = first_own + first_got.astype(F32)
    second_mine = second_own[0] + second_got_own.astype(F32)
    second_theirs = (second_other[0] + second_got_other.astype(F32)).astype(BF)
    first_sum = first_sum[0] + swap(first_sum[1].astype(BF), "row", 2).astype(F32)
    second_sum = second_mine + swap(second_theirs, "col", 1).astype(F32)
    yield jnp.concatenate([first_sum, second_sum], 0)


def order(*values):
    return lax.optimization_barrier(values)


class LineSum:
    def __init__(self):
        self.line = lax.axis_size("dp") == 4
        self.flight = []

    def add(self, values, finish):
        if self.line:
            self.flight.append([0, values, None, finish])
        else:
            if values.dtype == F32:
                finish(lax.psum(values, "dp"))
                return
            mine = lax.psum_scatter(values, "dp", scatter_dimension=0, tiled=True)
            finish(lax.all_gather(mine, "dp", axis=0, tiled=True))

    def step(self, *anchors):
        moving = [item for item in self.flight if item[2] is not None]
        results = order(*anchors, *[item[2] for item in moving])
        for item, got in zip(moving, results[len(anchors) :]):
            item[2] = got
        place = lax.axis_index("dp")
        for item in list(self.flight):
            stage, values, got, finish = item
            if stage == 3:
                finish(jnp.where((place == 0) | (place == 3), got, values))
                self.flight.remove(item)
                continue
            if stage:
                values = (values.astype(F32) + got.astype(F32)).astype(values.dtype)
            pairs = ([(0, 1), (3, 2)], [(1, 2), (2, 1)], [(1, 0), (2, 3)])[stage]
            item[:3] = [stage + 1, values, lax.ppermute(values, "dp", pairs)]
        return results[: len(anchors)]

    def drain(self):
        while self.flight:
            self.step()


def norm_forward(values, gain, full_width):
    squares = swap_sum(jnp.sum(values * values, -1, keepdims=True))
    scale = lax.rsqrt(squares / full_width + epsilon)
    normed = values * scale
    return (normed, scale, (normed * gain).astype(BF))


def norm_backward(grad_hidden, normed, scale, gain, full_width):
    grad_normed = grad_hidden * gain
    inner_sum = swap_sum(jnp.sum(grad_normed * normed, -1, keepdims=True))
    return (
        scale * (grad_normed - normed * inner_sum / full_width),
        jnp.sum(grad_hidden * normed, 0),
    )


def contract(leading, weight):
    return jnp.dot(leading, weight, preferred_element_type=F32)


def contract_flipped(leading, weight):
    return lax.dot_general(
        leading, weight, (((1,), (1,)), ((), ())), preferred_element_type=F32
    )


def outer_sum(leading, trailing):
    return lax.dot_general(
        leading, trailing, (((0,), (0,)), ((), ())), preferred_element_type=F32
    ).astype(BF)


ROWS = 256
PAIR = 2 * HD


def dot_nt(leading, trailing):
    return lax.dot_general(leading, trailing, (((1,), (1,)), ((), ())), preferred_element_type=F32)


def dot_nn(leading, trailing):
    return jnp.dot(leading, trailing, preferred_element_type=F32)


def turn(vectors, cosine, sine, lane):
    ahead = pltpu.roll(vectors, PAIR - HD // 2, 1)
    behind = pltpu.roll(vectors, HD // 2, 1)
    return vectors * cosine + jnp.where(lane % HD < HD // 2, ahead, behind) * sine


def fill_bias(starts_ref, bias):
    length = bias.shape[0]
    for base in range(0, length, ROWS):
        key = lax.broadcasted_iota(jnp.int32, (ROWS, length), 0) + base
        query = lax.broadcasted_iota(jnp.int32, (ROWS, length), 1)
        allowed = (key <= query) & (key >= starts_ref[0])
        bias[base : base + ROWS, :] = jnp.where(allowed, 0.0, -1e30)


def split_heads(values, lane):
    low = jnp.where(lane < HD, values, 0.0)
    return low, pltpu.roll(low, HD, 1)


def forward_kernel(
    kept_ref, sent_ref, kept_kv_ref, sent_kv_ref, cos_ref, sin_ref, starts_ref, *rest, anchors
):
    att_ref, q_ref, kv_ref, lse_ref, keys, values_t, bias = rest[anchors:]
    length = kept_ref.shape[0]
    lane = lax.broadcasted_iota(jnp.int32, (length, PAIR), 1)

    @pl.when(pl.program_id(1) == 0)
    def _():
        joined = kept_kv_ref[...].astype(F32) + sent_kv_ref[...].astype(F32)
        turned = turn(joined, cos_ref[0], sin_ref[0], lane)
        low = jnp.where(lane < HD, turned, joined).astype(BF)
        kv_ref[...] = low
        wide = low.astype(F32)
        key_a, key_b = split_heads(wide, lane)
        keys[0] = key_a.astype(BF)
        keys[1] = key_b.astype(BF)
        value_a, value_b = split_heads(pltpu.roll(wide, HD, 1), lane)
        values_t[0] = value_a.T.astype(BF)
        values_t[1] = value_b.T.astype(BF)
        fill_bias(starts_ref, bias)

    joined = kept_ref[...].astype(F32) + sent_ref[...].astype(F32)
    queries = turn(joined, cos_ref[0], sin_ref[0], lane).astype(BF)
    q_ref[...] = queries
    queries = queries * jnp.asarray(HD**-0.5, BF)
    for base in range(0, length, ROWS):
        block = queries[base : base + ROWS]
        count = base + ROWS
        mixed = jnp.zeros((PAIR, ROWS), F32)
        for head in range(2):
            scores = dot_nt(keys[head, :count], block) + bias[:count, base:count]
            highest = jnp.max(scores, 0, keepdims=True)
            weights = jnp.exp(scores - highest)
            total = jnp.sum(weights, 0, keepdims=True)
            part = dot_nn(values_t[head, :, :count], weights.astype(BF))
            mixed = mixed + part / total
            lse_ref[0, head : head + 1, base:count] = highest + jnp.log(total)
        att_ref[base:count, :] = mixed.T.astype(BF)


def backward_kernel(
    kept_ref, sent_ref, q_ref, kv_ref, lse_ref, cos_ref, sin_ref, starts_ref, *rest, anchors
):
    grad_ref, keys, keys_t, values, bias, grad_keys, grad_values = rest[anchors:]
    length = kv_ref.shape[0]
    lane = lax.broadcasted_iota(jnp.int32, (length, PAIR), 1)
    step = pl.program_id(1)
    last = pl.num_programs(1) - 1

    @pl.when(step == 0)
    def _():
        wide = kv_ref[...].astype(F32)
        for head, part in enumerate(split_heads(wide, lane)):
            keys[head] = part.astype(BF)
            keys_t[head] = part.T.astype(BF)
        for head, part in enumerate(split_heads(pltpu.roll(wide, HD, 1), lane)):
            values[head] = part.astype(BF)
        fill_bias(starts_ref, bias)
        grad_keys[...] = jnp.zeros_like(grad_keys)
        grad_values[...] = jnp.zeros_like(grad_values)

    @pl.when(step < last)
    def _():
        given = (kept_ref[...].astype(F32) + sent_ref[...].astype(F32)).astype(BF)
        queries = q_ref[...] * jnp.asarray(HD**-0.5, BF)
        zero = jnp.zeros_like(given)
        for base in range(0, length, ROWS):
            count = base + ROWS
            block = queries[base:count]
            gave = given[base:count]
            side = lane[base:count] < HD
            grad_t = jnp.zeros((PAIR, ROWS), F32)
            for head in range(2):
                mine = side if head == 0 else jnp.logical_not(side)
                block_mine = jnp.where(mine, block, zero[:ROWS])
                gave_mine = jnp.where(mine, gave, zero[:ROWS])
                scores = dot_nt(keys[head, :count], block) + bias[:count, base:count]
                weights = jnp.exp(scores - lse_ref[0, head : head + 1, base:count])
                grad_weights = dot_nt(values[head, :count], gave)
                product = weights * grad_weights
                inner = jnp.sum(product, 0, keepdims=True)
                grad_scores = (product - weights * inner).astype(BF)
                grad_values[:count] += dot_nn(weights.astype(BF), gave_mine)
                grad_keys[:count] += dot_nn(grad_scores, block_mine)
                grad_t = grad_t + dot_nn(keys_t[head, :, :count], grad_scores)
            grad = grad_t.T * HD**-0.5
            grad_ref[base:count, :] = turn(
                grad, cos_ref[0, base:count], -sin_ref[0, base:count], lane[base:count]
            ).astype(BF)

    @pl.when(step == last)
    def _():
        key_sum = grad_keys[...] + pltpu.roll(grad_keys[...], HD, 1)
        value_sum = grad_values[...] + pltpu.roll(grad_values[...], HD, 1)
        turned = turn(key_sum, cos_ref[0], -sin_ref[0], lane)
        grad_ref[...] = jnp.where(lane < HD, turned, value_sum).astype(BF)


VMEM = 48 * 1024 * 1024


def hidden_kernel(
    own_ref, other_ref, gate_ref, gate_other_ref, up_ref, up_other_ref, given_ref,
    act_ref, grad_gate_ref, grad_up_ref,
):
    own, other = own_ref[...], other_ref[...]
    gate = dot_nn(own, gate_ref[...]) + dot_nn(other, gate_other_ref[...])
    up = dot_nn(own, up_ref[...]) + dot_nn(other, up_other_ref[...])
    given = given_ref[...].astype(F32)
    bent = 1.0 / (1.0 + jnp.exp(-gate))
    silu = gate * bent
    act_ref[...] = (silu * up).astype(BF)
    grad_gate_ref[...] = (given * up * bent * (1.0 + gate * (1.0 - bent))).astype(BF)
    grad_up_ref[...] = (given * silu).astype(BF)


def hidden_part(own, other, gate, gate_other, up, up_other, given):
    tokens, width = own.shape
    hidden = gate.shape[1]
    rows = lambda columns: pl.BlockSpec((ROWS, columns), lambda i: (i, 0))
    whole = pl.BlockSpec((width, hidden), lambda i: (0, 0))
    return pl.pallas_call(
        hidden_kernel,
        grid=(tokens // ROWS,),
        in_specs=[rows(width), rows(width), whole, whole, whole, whole, rows(hidden)],
        out_specs=[rows(hidden)] * 3,
        out_shape=[jax.ShapeDtypeStruct((tokens, hidden), BF)] * 3,
        compiler_params=pltpu.CompilerParams(vmem_limit_bytes=VMEM),
        cost_estimate=pl.CostEstimate(
            flops=8 * tokens * width * hidden, bytes_accessed=24 * 2**20, transcendentals=0
        ),
        name="hidden_part",
    )(own, other, gate, gate_other, up, up_other, given)


def back_kernel(grad_gate_ref, grad_up_ref, gate_ref, gate_other_ref, up_ref, up_other_ref, own_ref, other_ref):
    grad_gate, grad_up = grad_gate_ref[...], grad_up_ref[...]
    own_ref[...] = (dot_nt(grad_gate, gate_ref[...]) + dot_nt(grad_up, up_ref[...])).astype(BF)
    other_ref[...] = (
        dot_nt(grad_gate, gate_other_ref[...]) + dot_nt(grad_up, up_other_ref[...])
    ).astype(BF)


def back_part(grad_gate, grad_up, gate, gate_other, up, up_other, half):
    hidden = grad_gate.shape[1]
    tokens = grad_gate.shape[0] // 2
    width = gate.shape[0]
    steps = tokens // ROWS
    rows = pl.BlockSpec((ROWS, hidden), lambda i: (i + half * steps, 0))
    whole = pl.BlockSpec((width, hidden), lambda i: (0, 0))
    return pl.pallas_call(
        back_kernel,
        grid=(steps,),
        in_specs=[rows, rows, whole, whole, whole, whole],
        out_specs=[pl.BlockSpec((ROWS, width), lambda i: (i, 0))] * 2,
        out_shape=[jax.ShapeDtypeStruct((tokens, width), BF)] * 2,
        compiler_params=pltpu.CompilerParams(vmem_limit_bytes=VMEM),
        cost_estimate=pl.CostEstimate(
            flops=8 * tokens * width * hidden, bytes_accessed=12 * 2**20, transcendentals=0
        ),
        name="back_part",
    )(grad_gate, grad_up, gate, gate_other, up, up_other)


def attention_forward(kept, sent, cosine, sine, starts, anchors=()):
    sequences, _, length = starts.shape
    pairs = kept.shape[1] // PAIR - 1
    here = lambda s, i: (s, i)
    kv_at = lambda s, i: (s, pairs)
    table = pl.BlockSpec((1, length, PAIR), lambda s, i: (s, 0, 0))
    return pl.pallas_call(
        lambda *refs: forward_kernel(*refs, anchors=len(anchors)),
        grid=(sequences, pairs),
        in_specs=[
            pl.BlockSpec((length, PAIR), here),
            pl.BlockSpec((length, PAIR), here),
            pl.BlockSpec((length, PAIR), kv_at),
            pl.BlockSpec((length, PAIR), kv_at),
            table,
            table,
            pl.BlockSpec((1, 1, length), lambda s, i: (s, 0, 0)),
        ]
        + [pl.BlockSpec(memory_space=pl.ANY)] * len(anchors),
        out_specs=[
            pl.BlockSpec((length, PAIR), here),
            pl.BlockSpec((length, PAIR), here),
            pl.BlockSpec((length, PAIR), lambda s, i: (s, 0)),
            pl.BlockSpec((1, 2, length), lambda s, i: (s * pairs + i, 0, 0)),
        ],
        out_shape=[
            jax.ShapeDtypeStruct((sequences * length, pairs * PAIR), BF),
            jax.ShapeDtypeStruct((sequences * length, pairs * PAIR), BF),
            jax.ShapeDtypeStruct((sequences * length, PAIR), BF),
            jax.ShapeDtypeStruct((sequences * pairs, 2, length), F32),
        ],
        scratch_shapes=[
            pltpu.VMEM((2, length, PAIR), BF),
            pltpu.VMEM((2, PAIR, length), BF),
            pltpu.VMEM((length, length), F32),
        ],
        compiler_params=pltpu.CompilerParams(vmem_limit_bytes=VMEM),
        cost_estimate=pl.CostEstimate(
            flops=20 * 10**9, bytes_accessed=8 * 2**20, transcendentals=0
        ),
        name="attention_forward",
    )(kept, sent, kept, sent, cosine, sine, starts, *anchors)


def attention_backward(kept, sent, queries, kv, log_totals, cosine, sine, starts, anchors=()):
    sequences, _, length = starts.shape
    pairs = queries.shape[1] // PAIR
    here = lambda s, i: (s, jnp.minimum(i, pairs - 1))
    table = pl.BlockSpec((1, length, PAIR), lambda s, i: (s, 0, 0))
    return pl.pallas_call(
        lambda *refs: backward_kernel(*refs, anchors=len(anchors)),
        grid=(sequences, pairs + 1),
        in_specs=[
            pl.BlockSpec((length, PAIR), here),
            pl.BlockSpec((length, PAIR), here),
            pl.BlockSpec((length, PAIR), here),
            pl.BlockSpec((length, PAIR), lambda s, i: (s, 0)),
            pl.BlockSpec(
                (1, 2, length), lambda s, i: (s * pairs + jnp.minimum(i, pairs - 1), 0, 0)
            ),
            table,
            table,
            pl.BlockSpec((1, 1, length), lambda s, i: (s, 0, 0)),
        ]
        + [pl.BlockSpec(memory_space=pl.ANY)] * len(anchors),
        out_specs=pl.BlockSpec((length, PAIR), lambda s, i: (s, i)),
        out_shape=jax.ShapeDtypeStruct((sequences * length, (pairs + 1) * PAIR), BF),
        scratch_shapes=[
            pltpu.VMEM((2, length, PAIR), BF),
            pltpu.VMEM((2, PAIR, length), BF),
            pltpu.VMEM((2, length, PAIR), BF),
            pltpu.VMEM((length, length), F32),
            pltpu.VMEM((length, PAIR), F32),
            pltpu.VMEM((length, PAIR), F32),
        ],
        compiler_params=pltpu.CompilerParams(vmem_limit_bytes=VMEM),
        cost_estimate=pl.CostEstimate(
            flops=40 * 10**9, bytes_accessed=8 * 2**20, transcendentals=0
        ),
        name="attention_backward",
    )(kept, sent, queries, kv, log_totals, cosine, sine, starts, *anchors)


def body(
    inputs,
    segments,
    norm1_gain,
    query_weight,
    key_weight,
    value_weight,
    out_weight,
    norm2_gain,
    gate_weight,
    up_weight,
    down_weight,
    cotangent,
):
    columns = lax.axis_size("col")
    full_width = norm1_gain.shape[0] * columns
    query_width = query_weight.shape[1]
    pair_width = key_weight.shape[1]
    hidden_width = gate_weight.shape[1]
    per_column = segments.shape[0] // columns
    seq_length = segments.shape[1]
    local_tokens = per_column * seq_length
    column = lax.axis_index("col")
    first_column = column == 0
    part = hidden_width // 2
    line = LineSum()

    def cut(weight, axis):
        low = lax.slice_in_dim(weight, 0, part, axis=axis)
        high = lax.slice_in_dim(weight, part, 2 * part, axis=axis)
        return jnp.where(first_column, low, high), jnp.where(first_column, high, low)

    even = lax.axis_size("dp") % 2 == 0
    low_plane = (lax.axis_index("dp") & 1) == 0

    def cross(sent):
        if not even:
            return swap(sent, "col", 1)
        half = sent.shape[0] // 2
        return swap(jnp.where(low_plane, sent[:half], sent[half:]), "col", 1)

    def share(got):
        if not even:
            return got
        return pair_up(got, swap(got, "dp", 1), low_plane, 0)

    def rows_of(whole, index):
        return lax.dynamic_slice_in_dim(whole, index * local_tokens, local_tokens, 0)

    def gather_col(block):
        return pair_up(block, swap(block, "col", 1), first_column, 0)

    features = inputs.astype(F32)
    gain_one = norm1_gain.astype(F32)
    gain_two = norm2_gain.astype(F32)
    normed_one, scale_one, hidden_one = norm_forward(features, gain_one, full_width)
    hidden_one_all = gather_row(hidden_one)
    gate, gate_sent = cut(gate_weight, 1)
    up, up_sent = cut(up_weight, 1)
    down, down_sent = cut(down_weight, 0)
    gate_got, down_got, up_got = cross(gate_sent), cross(down_sent), cross(up_sent)

    qkv_weight = jnp.concatenate([query_weight, key_weight, value_weight], 1)
    local_segments = lax.dynamic_slice_in_dim(segments, column * per_column, per_column, 0)
    positions = jax.vmap(positions_of)(local_segments)
    cosine, sine = rotary_tables(positions)
    starts = (jnp.arange(seq_length, dtype=jnp.int32) - positions)[:, None, :]

    hidden_one_all, gate_got = order(hidden_one_all, gate_got)
    leaving = contract(rows_of(hidden_one_all, 1 - column), qkv_weight).astype(BF)
    leaving, cotangent, down_got, up_got = order(leaving, cotangent, down_got, up_got)
    sent = swap(leaving, "col", 1)
    kept = contract(rows_of(hidden_one_all, column), qkv_weight)
    cot_plane = gather_plane(cotangent)
    cot_flight = next(cot_plane)
    kept, sent, *cot_flight = order(kept, sent, *cot_flight)
    cot_flight = cot_plane.send(cot_flight)
    gate_other, down_other, up_other = share(gate_got), share(down_got), share(up_got)
    attended, queries, kv, log_totals = attention_forward(kept, sent, cosine, sine, starts)
    attended, gate_other, down_other, *cot_flight = order(
        attended, gate_other, down_other, *cot_flight
    )
    cot_own, cot_other = cot_plane.send(cot_flight)
    attended_all = gather_col(attended)
    attended_all, up_other, cot_own, cot_other = order(attended_all, up_other, cot_own, cot_other)
    attn_branch = scatter_row(attended_all, lambda rows: contract(rows, out_weight))
    grad_activated = (
        contract_flipped(cot_own, down) + contract_flipped(cot_other, down_other)
    ).astype(BF)
    attn_branch, grad_activated = order(attn_branch, grad_activated)
    middle = features + attn_branch
    normed_two, scale_two, hidden_two = norm_forward(middle, gain_two, full_width)
    two_plane = gather_plane(hidden_two)
    two_own, two_other = two_plane.send(two_plane.send(next(two_plane)))
    activated, grad_gate_part, grad_up_part = hidden_part(
        two_own, two_other, gate, gate_other, up, up_other, grad_activated
    )

    done = {}

    def reduce(name, values):
        line.add(values, lambda total: done.__setitem__(name, total))

    down_grad = outer_sum(activated, cot_own)
    grad_gate_part, grad_up_part, down_grad = order(grad_gate_part, grad_up_part, down_grad)
    reduce("down_own", down_grad)
    line.step()
    leaving = back_part(grad_gate_part, grad_up_part, gate, gate_other, up, up_other, 1)
    down_away = outer_sum(activated, cot_other)
    *leaving, down_away = order(*leaving, down_away)
    down_away = swap(down_away, "col", 1)
    staying = back_part(grad_gate_part, grad_up_part, gate, gate_other, up, up_other, 0)
    plane = scatter_plane(staying, leaving)
    flight = next(plane)
    gate_grad = outer_sum(grad_gate_part, two_own)
    up_grad = outer_sum(grad_up_part, two_own)
    gate_other_grad = outer_sum(grad_gate_part, two_other)
    reduce("gate_own", gate_grad)
    *flight, up_grad, gate_other_grad = line.step(*flight, up_grad, gate_other_grad)
    grad_hidden_two = plane.send(flight)
    up_other_grad = outer_sum(grad_up_part, two_other)
    grad_hidden_two, up_other_grad = order(grad_hidden_two, up_other_grad)
    grad_norm_two, grad_gain_two = norm_backward(
        grad_hidden_two, normed_two, scale_two, gain_two, full_width
    )
    grad_middle = cotangent.astype(F32) + grad_norm_two
    branch_low = grad_middle.astype(BF)
    reduce("down_other", down_away)
    branch_low, gate_other_grad = line.step(branch_low, gate_other_grad)
    gate_away = swap(gate_other_grad, "col", 1)
    branch_all = gather_row(branch_low)
    reduce("up_own", up_grad)
    branch_all, gate_away = line.step(branch_all, gate_away)
    leaving = contract_flipped(rows_of(branch_all, 1 - column), out_weight).astype(BF)
    grad_sent = swap(leaving, "col", 1)
    grad_kept = contract_flipped(rows_of(branch_all, column), out_weight)
    out_grad = outer_sum(attended_all, branch_all)
    reduce("gate_other", gate_away)
    grad_sent, out_grad, up_other_grad = line.step(grad_sent, out_grad, up_other_grad)
    up_away = swap(up_other_grad, "col", 1)
    grad_projected = attention_backward(
        grad_kept, grad_sent, queries, kv, log_totals, cosine, sine, starts
    )
    reduce("out", out_grad)
    (grad_projected,) = line.step(grad_projected)
    projected_got = swap(grad_projected, "col", 1)
    lower = activated.shape[0] // 2
    out_staying = [contract(activated[:lower], weight).astype(BF) for weight in (down, down_other)]
    out_leaving = [contract(activated[lower:], weight).astype(BF) for weight in (down, down_other)]
    reduce("up_other", up_away)
    projected_got, *out_parts = line.step(projected_got, *out_staying, *out_leaving)
    out_plane = scatter_plane(out_parts[:2], out_parts[2:])
    out_flight = next(out_plane)
    projected_all = pair_up(grad_projected, projected_got, first_column, 0)
    qkv_grad = outer_sum(hidden_one_all, projected_all)
    grad_hidden_one = scatter_row(projected_all, lambda rows: contract_flipped(rows, qkv_weight))
    reduce("qkv", qkv_grad)
    (grad_hidden_one,) = line.step(grad_hidden_one)
    grad_norm_one, grad_gain_one = norm_backward(
        grad_hidden_one, normed_one, scale_one, gain_one, full_width
    )
    grad_inputs = grad_middle + grad_norm_one
    gain_grads = jnp.stack([grad_gain_one, grad_gain_two])
    bit = 1
    while bit < lax.axis_size("row"):
        gain_grads = gain_grads + swap(gain_grads, "row", bit)
        bit *= 2
    reduce("gains", gain_grads)
    out_flight = line.step(*out_flight, grad_inputs)
    grad_inputs = out_flight[3]
    branch = out_plane.send(out_flight[:3])
    (branch,) = line.step(branch)
    outputs = (middle + branch).astype(BF)
    line.drain()

    def rows_in(name):
        return pair_up(done[name + "_own"], done[name + "_other"], first_column, 0)

    grad_gate = rows_in("gate").T.astype(F32)
    grad_up = rows_in("up").T.astype(F32)
    grad_down = rows_in("down").astype(F32)
    grad_out = done["out"].astype(F32)
    grad_qkv = done["qkv"].astype(F32)
    gain_grads = done["gains"]
    return (
        outputs,
        grad_inputs,
        gain_grads[0],
        grad_qkv[:, :query_width],
        grad_qkv[:, query_width : query_width + pair_width],
        grad_qkv[:, query_width + pair_width :],
        grad_out,
        gain_grads[1],
        grad_gate,
        grad_up,
        grad_down,
    )


def solution(mesh):
    in_specs = (
        P(("dp", "row"), "col"),
        P("dp", None),
        P("col"),
        P("col", "row"),
        P("col", "row"),
        P("col", "row"),
        P("row", "col"),
        P("col"),
        P("col", "row"),
        P("col", "row"),
        P("row", "col"),
        P(("dp", "row"), "col"),
    )
    out_specs = (
        P(("dp", "row"), "col"),
        P(("dp", "row"), "col"),
        P("col"),
        P("col", "row"),
        P("col", "row"),
        P("col", "row"),
        P("row", "col"),
        P("col"),
        P("col", "row"),
        P("col", "row"),
        P("row", "col"),
    )
    return jax.shard_map(body, mesh=mesh, in_specs=in_specs, out_specs=out_specs, check_vma=False)
```

```python
import jax
import jax.numpy as jnp
from jax import lax
from jax.experimental import pallas as pl
from jax.experimental.pallas import tpu as pltpu
from jax.sharding import PartitionSpec as P

HD = 64
LANES = 128

epsilon = 1e-05
rope_base = 10000.0
BF = jnp.bfloat16
F32 = jnp.float32


def positions_of(segment_row):
    indices = jnp.arange(segment_row.shape[0], dtype=jnp.int32)
    previous = jnp.concatenate([segment_row[:1] - 1, segment_row[:-1]])
    start_index = lax.cummax(jnp.where(segment_row != previous, indices, 0), axis=0)
    return indices - start_index


def rotary_tables(positions):
    frequency = rope_base ** (-jnp.arange(HD // 2).astype(F32) * 2.0 / HD)
    angles = positions.astype(F32)[..., None] * frequency
    cosine = jnp.cos(angles)
    sine = jnp.sin(angles)
    return (
        jnp.concatenate([cosine] * 4, -1),
        jnp.concatenate([-sine, sine, -sine, sine], -1),
    )


def swap(values, axis, bit):
    pairs = [(i, i ^ bit) for i in range(lax.axis_size(axis))]
    return lax.ppermute(values, axis, pairs)


def swap_sum(values):
    return values + swap(values, "col", 1)


def pick(values, index, axis):
    return lax.dynamic_index_in_dim(values, index, axis, keepdims=False)


def pair_up(own, other, first, axis):
    return jnp.concatenate([jnp.where(first, own, other), jnp.where(first, other, own)], axis)


def gather_row(block, between=lambda far: far):
    me = lax.axis_index("row")
    far = swap(block, "row", 2)
    sibling = swap(block, "row", 1)
    far = between(far)
    even = (me & 1) == 0
    near_pair = pair_up(block, sibling, even, 0)
    far_pair = pair_up(far, swap(far, "row", 1), even, 0)
    mine = (me >> 1) == lax.axis_index("col")
    return jnp.where(mine, near_pair, far_pair), jnp.where(mine, far_pair, near_pair)


def scatter_row(sequences, product):
    me = lax.axis_index("row")
    parity = me & 1
    block = sequences[0].shape[0] // 2

    def rows(index):
        parts = [lax.dynamic_slice_in_dim(rows, index * block, block, 0) for rows in sequences]
        return jnp.concatenate(parts, 0)

    sent = product(rows(1 - parity)).astype(BF)
    arrived = swap(sent, "row", 1)
    kept = product(rows(parity))
    both = (kept + arrived.astype(F32)).reshape(2, block, -1)
    where = (me >> 1) ^ lax.axis_index("col")
    return pick(both, where, 0) + swap(pick(both, 1 - where, 0).astype(BF), "row", 2).astype(F32)


def gather_plane(block):
    half = block.shape[0] // 2
    across, along = swap(block, "col", 1), swap(block, "row", 2)
    corner = swap(along[:half], "col", 1), swap(across[half:], "row", 2)
    own = jnp.concatenate([block, along], 0)
    other = jnp.concatenate([across, *corner], 0)
    return (own, swap(own, "row", 1)), (other, swap(other, "row", 1))


def scatter_plane(kept, sent):
    arrived = [swap(values, "row", 1) for values in sent]
    own, other = [
        (values.astype(F32) + more.astype(F32)).reshape(2, -1, values.shape[1])
        for values, more in zip(kept, arrived)
    ]
    half = own.shape[1] // 2
    first_own, first_other = own[:, :half], other[:, :half].astype(BF)
    second_own, second_other = own[0, half:], other[0, half:]
    leaving = first_other, own[1, half:].astype(BF), other[1, half:].astype(BF)
    leaving = yield leaving
    got = swap(leaving[0], "col", 1), swap(leaving[1], "row", 2), swap(leaving[2], "row", 2)
    first_got, second_got_own, second_got_other = yield got
    first_sum = first_own + first_got.astype(F32)
    second_mine = second_own + second_got_own.astype(F32)
    second_theirs = (second_other + second_got_other.astype(F32)).astype(BF)
    first_sum = first_sum[0] + swap(first_sum[1].astype(BF), "row", 2).astype(F32)
    second_sum = second_mine + swap(second_theirs, "col", 1).astype(F32)
    yield jnp.concatenate([first_sum, second_sum], 0)


def scatter_late(own, across):
    both = (own + across.astype(F32)).reshape(2, -1, own.shape[1])
    return both[0] + swap(both[1].astype(BF), "row", 2).astype(F32)


def order(*values):
    return lax.optimization_barrier(values)


class LineSum:
    stages = ([(0, 1), (3, 2)], [(1, 2), (2, 1)], [(1, 0), (2, 3)])

    def __init__(self):
        self.line = lax.axis_size("dp") == 4
        self.flight = []

    def add(self, values, finish):
        if self.line:
            self.flight.append([1, values, lax.ppermute(values, "dp", self.stages[0]), finish])
        else:
            mine = lax.psum_scatter(values, "dp", scatter_dimension=0, tiled=True)
            finish(lax.all_gather(mine, "dp", axis=0, tiled=True))

    def step(self, *anchors, late=()):
        moving = list(self.flight)
        results = order(*anchors, *late, *[item[2] for item in moving])
        kept, late, got = (
            results[: len(anchors)],
            results[len(anchors) : len(anchors) + len(late)],
            results[len(anchors) + len(late) :],
        )
        place = lax.axis_index("dp")
        going = []
        for item, arrived in zip(moving, got):
            stage, values, _, finish = item
            if stage == 3:
                finish(jnp.where((place == 0) | (place == 3), arrived, values))
                self.flight.remove(item)
                continue
            item[1] = (values.astype(F32) + arrived.astype(F32)).astype(values.dtype)
            going.append(item)
        if late:
            results = order(*late, *[item[1] for item in going])
            late = results[: len(late)]
            for item, values in zip(going, results[len(late) :]):
                item[1] = values
        for item in going:
            item[2] = lax.ppermute(item[1], "dp", self.stages[item[0]])
            item[0] += 1
        return (*kept, *late)

    def drain(self):
        while self.flight:
            self.step()


def norm_forward(values, gain, full_width):
    squares = swap_sum(jnp.sum(values * values, -1, keepdims=True))
    scale = lax.rsqrt(squares / full_width + epsilon)
    normed = values * scale
    return (normed, scale, (normed * gain).astype(BF))


def norm_backward(grad_hidden, normed, scale, gain, full_width):
    grad_normed = grad_hidden * gain
    inner_sum = swap_sum(jnp.sum(grad_normed * normed, -1, keepdims=True))
    return (
        scale * (grad_normed - normed * inner_sum / full_width),
        jnp.sum(grad_hidden * normed, 0),
    )


def contract(leading, weight):
    return jnp.dot(leading, weight, preferred_element_type=F32)


def contract_flipped(leading, weight):
    return lax.dot_general(
        leading, weight, (((1,), (1,)), ((), ())), preferred_element_type=F32
    )


def outer_sum(leading, trailing):
    return lax.dot_general(
        leading, trailing, (((0,), (0,)), ((), ())), preferred_element_type=F32
    ).astype(BF)


ROWS = 256
PAIR = 2 * HD


def dot_nt(leading, trailing):
    return lax.dot_general(leading, trailing, (((1,), (1,)), ((), ())), preferred_element_type=F32)


def dot_nn(leading, trailing):
    return jnp.dot(leading, trailing, preferred_element_type=F32)


def turn(vectors, cosine, sine, lane):
    ahead = pltpu.roll(vectors, PAIR - HD // 2, 1)
    behind = pltpu.roll(vectors, HD // 2, 1)
    return vectors * cosine + jnp.where(lane % HD < HD // 2, ahead, behind) * sine


def fill_bias(starts_ref, bias):
    length = bias.shape[0]
    for base in range(0, length, ROWS):
        key = lax.broadcasted_iota(jnp.int32, (ROWS, length), 0) + base
        query = lax.broadcasted_iota(jnp.int32, (ROWS, length), 1)
        allowed = (key <= query) & (key >= starts_ref[0])
        bias[base : base + ROWS, :] = jnp.where(allowed, 0.0, -1e30)


def split_heads(values, lane):
    low = jnp.where(lane < HD, values, 0.0)
    return low, pltpu.roll(low, HD, 1)


def forward_kernel(
    kept_ref, sent_ref, kept_kv_ref, sent_kv_ref, cos_ref, sin_ref, starts_ref, *rest, anchors
):
    att_ref, q_ref, kv_ref, lse_ref, keys, values_t, bias = rest[anchors:]
    length = kept_ref.shape[0]
    lane = lax.broadcasted_iota(jnp.int32, (length, PAIR), 1)

    @pl.when(pl.program_id(1) == 0)
    def _():
        joined = kept_kv_ref[...].astype(F32) + sent_kv_ref[...].astype(F32)
        turned = turn(joined, cos_ref[0], sin_ref[0], lane)
        low = jnp.where(lane < HD, turned, joined).astype(BF)
        kv_ref[...] = low
        wide = low.astype(F32)
        key_a, key_b = split_heads(wide, lane)
        keys[0] = key_a.astype(BF)
        keys[1] = key_b.astype(BF)
        value_a, value_b = split_heads(pltpu.roll(wide, HD, 1), lane)
        values_t[0] = value_a.T.astype(BF)
        values_t[1] = value_b.T.astype(BF)
        fill_bias(starts_ref, bias)

    joined = kept_ref[...].astype(F32) + sent_ref[...].astype(F32)
    queries = turn(joined, cos_ref[0], sin_ref[0], lane).astype(BF)
    q_ref[...] = queries
    queries = queries * jnp.asarray(HD**-0.5, BF)
    for base in range(0, length, ROWS):
        block = queries[base : base + ROWS]
        count = base + ROWS
        mixed = jnp.zeros((PAIR, ROWS), F32)
        for head in range(2):
            scores = dot_nt(keys[head, :count], block) + bias[:count, base:count]
            highest = jnp.max(scores, 0, keepdims=True)
            weights = jnp.exp(scores - highest)
            total = jnp.sum(weights, 0, keepdims=True)
            part = dot_nn(values_t[head, :, :count], weights.astype(BF))
            mixed = mixed + part / total
            lse_ref[0, head : head + 1, base:count] = highest + jnp.log(total)
        att_ref[base:count, :] = mixed.T.astype(BF)


def backward_kernel(
    kept_ref, sent_ref, q_ref, kv_ref, lse_ref, cos_ref, sin_ref, starts_ref, *rest, anchors
):
    grad_ref, keys, keys_t, values, bias, grad_keys, grad_values = rest[anchors:]
    length = kv_ref.shape[0]
    lane = lax.broadcasted_iota(jnp.int32, (length, PAIR), 1)
    step = pl.program_id(1)
    last = pl.num_programs(1) - 1

    @pl.when(step == 0)
    def _():
        wide = kv_ref[...].astype(F32)
        for head, part in enumerate(split_heads(wide, lane)):
            keys[head] = part.astype(BF)
            keys_t[head] = part.T.astype(BF)
        for head, part in enumerate(split_heads(pltpu.roll(wide, HD, 1), lane)):
            values[head] = part.astype(BF)
        fill_bias(starts_ref, bias)
        grad_keys[...] = jnp.zeros_like(grad_keys)
        grad_values[...] = jnp.zeros_like(grad_values)

    @pl.when(step < last)
    def _():
        given = (kept_ref[...].astype(F32) + sent_ref[...].astype(F32)).astype(BF)
        queries = q_ref[...] * jnp.asarray(HD**-0.5, BF)
        zero = jnp.zeros_like(given)
        for base in range(0, length, ROWS):
            count = base + ROWS
            block = queries[base:count]
            gave = given[base:count]
            side = lane[base:count] < HD
            grad_t = jnp.zeros((PAIR, ROWS), F32)
            for head in range(2):
                mine = side if head == 0 else jnp.logical_not(side)
                block_mine = jnp.where(mine, block, zero[:ROWS])
                gave_mine = jnp.where(mine, gave, zero[:ROWS])
                scores = dot_nt(keys[head, :count], block) + bias[:count, base:count]
                weights = jnp.exp(scores - lse_ref[0, head : head + 1, base:count])
                grad_weights = dot_nt(values[head, :count], gave)
                product = weights * grad_weights
                inner = jnp.sum(product, 0, keepdims=True)
                grad_scores = (product - weights * inner).astype(BF)
                grad_values[:count] += dot_nn(weights.astype(BF), gave_mine)
                grad_keys[:count] += dot_nn(grad_scores, block_mine)
                grad_t = grad_t + dot_nn(keys_t[head, :, :count], grad_scores)
            grad = grad_t.T * HD**-0.5
            grad_ref[base:count, :] = turn(
                grad, cos_ref[0, base:count], -sin_ref[0, base:count], lane[base:count]
            ).astype(BF)

    @pl.when(step == last)
    def _():
        key_sum = grad_keys[...] + pltpu.roll(grad_keys[...], HD, 1)
        value_sum = grad_values[...] + pltpu.roll(grad_values[...], HD, 1)
        turned = turn(key_sum, cos_ref[0], -sin_ref[0], lane)
        grad_ref[...] = jnp.where(lane < HD, turned, value_sum).astype(BF)


VMEM = 48 * 1024 * 1024


def hidden_kernel(
    own_ref, own_sibling_ref, other_ref, other_sibling_ref,
    gate_ref, gate_other_ref, up_ref, up_other_ref, given_ref,
    act_ref, grad_gate_ref, grad_up_ref,
):
    def tile(own_ref, other_ref):
        own, other = own_ref[...], other_ref[...]
        gate = dot_nn(own, gate_ref[...]) + dot_nn(other, gate_other_ref[...])
        up = dot_nn(own, up_ref[...]) + dot_nn(other, up_other_ref[...])
        given = given_ref[...].astype(F32)
        bent = 1.0 / (1.0 + jnp.exp(-gate))
        silu = gate * bent
        act_ref[...] = (silu * up).astype(BF)
        grad_gate_ref[...] = (given * up * bent * (1.0 + gate * (1.0 - bent))).astype(BF)
        grad_up_ref[...] = (given * silu).astype(BF)

    near = pl.program_id(0) < pl.num_programs(0) // 2

    @pl.when(near)
    def _():
        tile(own_ref, other_ref)

    @pl.when(jnp.logical_not(near))
    def _():
        tile(own_sibling_ref, other_sibling_ref)


def hidden_part(own, other, gate, gate_other, up, up_other, given):
    tokens, hidden = given.shape
    width = gate.shape[0]
    half = tokens // ROWS // 2
    rows = pl.BlockSpec((ROWS, hidden), lambda i: (i, 0))
    near = pl.BlockSpec((ROWS, width), lambda i: (jnp.minimum(i, half - 1), 0))
    sibling = pl.BlockSpec((ROWS, width), lambda i: (jnp.maximum(i - half, 0), 0))
    whole = pl.BlockSpec((width, hidden), lambda i: (0, 0))
    return pl.pallas_call(
        hidden_kernel,
        grid=(2 * half,),
        in_specs=[near, sibling, near, sibling, whole, whole, whole, whole, rows],
        out_specs=[rows] * 3,
        out_shape=[jax.ShapeDtypeStruct((tokens, hidden), BF)] * 3,
        compiler_params=pltpu.CompilerParams(vmem_limit_bytes=VMEM),
        cost_estimate=pl.CostEstimate(
            flops=8 * tokens * width * hidden, bytes_accessed=24 * 2**20, transcendentals=0
        ),
        name="hidden_part",
    )(*own, *other, gate, gate_other, up, up_other, given)


def back_kernel(grad_gate_ref, grad_up_ref, gate_ref, gate_other_ref, up_ref, up_other_ref, own_ref, other_ref):
    grad_gate, grad_up = grad_gate_ref[...], grad_up_ref[...]
    own_ref[...] = (dot_nt(grad_gate, gate_ref[...]) + dot_nt(grad_up, up_ref[...])).astype(BF)
    other_ref[...] = (
        dot_nt(grad_gate, gate_other_ref[...]) + dot_nt(grad_up, up_other_ref[...])
    ).astype(BF)


def back_part(grad_gate, grad_up, gate, gate_other, up, up_other, half):
    hidden = grad_gate.shape[1]
    tokens = grad_gate.shape[0] // 2
    width = gate.shape[0]
    steps = tokens // ROWS
    rows = pl.BlockSpec((ROWS, hidden), lambda i: (i + half * steps, 0))
    whole = pl.BlockSpec((width, hidden), lambda i: (0, 0))
    return pl.pallas_call(
        back_kernel,
        grid=(steps,),
        in_specs=[rows, rows, whole, whole, whole, whole],
        out_specs=[pl.BlockSpec((ROWS, width), lambda i: (i, 0))] * 2,
        out_shape=[jax.ShapeDtypeStruct((tokens, width), BF)] * 2,
        compiler_params=pltpu.CompilerParams(vmem_limit_bytes=VMEM),
        cost_estimate=pl.CostEstimate(
            flops=8 * tokens * width * hidden, bytes_accessed=12 * 2**20, transcendentals=0
        ),
        name="back_part",
    )(grad_gate, grad_up, gate, gate_other, up, up_other)


def attention_forward(kept, sent, cosine, sine, starts, anchors=()):
    sequences, _, length = starts.shape
    pairs = kept.shape[1] // PAIR - 1
    here = lambda s, i: (s, i)
    kv_at = lambda s, i: (s, pairs)
    table = pl.BlockSpec((1, length, PAIR), lambda s, i: (s, 0, 0))
    return pl.pallas_call(
        lambda *refs: forward_kernel(*refs, anchors=len(anchors)),
        grid=(sequences, pairs),
        in_specs=[
            pl.BlockSpec((length, PAIR), here),
            pl.BlockSpec((length, PAIR), here),
            pl.BlockSpec((length, PAIR), kv_at),
            pl.BlockSpec((length, PAIR), kv_at),
            table,
            table,
            pl.BlockSpec((1, 1, length), lambda s, i: (s, 0, 0)),
        ]
        + [pl.BlockSpec(memory_space=pl.ANY)] * len(anchors),
        out_specs=[
            pl.BlockSpec((length, PAIR), here),
            pl.BlockSpec((length, PAIR), here),
            pl.BlockSpec((length, PAIR), lambda s, i: (s, 0)),
            pl.BlockSpec((1, 2, length), lambda s, i: (s * pairs + i, 0, 0)),
        ],
        out_shape=[
            jax.ShapeDtypeStruct((sequences * length, pairs * PAIR), BF),
            jax.ShapeDtypeStruct((sequences * length, pairs * PAIR), BF),
            jax.ShapeDtypeStruct((sequences * length, PAIR), BF),
            jax.ShapeDtypeStruct((sequences * pairs, 2, length), F32),
        ],
        scratch_shapes=[
            pltpu.VMEM((2, length, PAIR), BF),
            pltpu.VMEM((2, PAIR, length), BF),
            pltpu.VMEM((length, length), F32),
        ],
        compiler_params=pltpu.CompilerParams(vmem_limit_bytes=VMEM),
        cost_estimate=pl.CostEstimate(
            flops=20 * 10**9, bytes_accessed=8 * 2**20, transcendentals=0
        ),
        name="attention_forward",
    )(kept, sent, kept, sent, cosine, sine, starts, *anchors)


def attention_backward(kept, sent, queries, kv, log_totals, cosine, sine, starts, anchors=()):
    sequences, _, length = starts.shape
    pairs = queries.shape[1] // PAIR
    here = lambda s, i: (s, jnp.minimum(i, pairs - 1))
    table = pl.BlockSpec((1, length, PAIR), lambda s, i: (s, 0, 0))
    return pl.pallas_call(
        lambda *refs: backward_kernel(*refs, anchors=len(anchors)),
        grid=(sequences, pairs + 1),
        in_specs=[
            pl.BlockSpec((length, PAIR), here),
            pl.BlockSpec((length, PAIR), here),
            pl.BlockSpec((length, PAIR), here),
            pl.BlockSpec((length, PAIR), lambda s, i: (s, 0)),
            pl.BlockSpec(
                (1, 2, length), lambda s, i: (s * pairs + jnp.minimum(i, pairs - 1), 0, 0)
            ),
            table,
            table,
            pl.BlockSpec((1, 1, length), lambda s, i: (s, 0, 0)),
        ]
        + [pl.BlockSpec(memory_space=pl.ANY)] * len(anchors),
        out_specs=pl.BlockSpec((length, PAIR), lambda s, i: (s, i)),
        out_shape=jax.ShapeDtypeStruct((sequences * length, (pairs + 1) * PAIR), BF),
        scratch_shapes=[
            pltpu.VMEM((2, length, PAIR), BF),
            pltpu.VMEM((2, PAIR, length), BF),
            pltpu.VMEM((2, length, PAIR), BF),
            pltpu.VMEM((length, length), F32),
            pltpu.VMEM((length, PAIR), F32),
            pltpu.VMEM((length, PAIR), F32),
        ],
        compiler_params=pltpu.CompilerParams(vmem_limit_bytes=VMEM),
        cost_estimate=pl.CostEstimate(
            flops=40 * 10**9, bytes_accessed=8 * 2**20, transcendentals=0
        ),
        name="attention_backward",
    )(kept, sent, queries, kv, log_totals, cosine, sine, starts, *anchors)


def body(
    inputs,
    segments,
    norm1_gain,
    query_weight,
    key_weight,
    value_weight,
    out_weight,
    norm2_gain,
    gate_weight,
    up_weight,
    down_weight,
    cotangent,
):
    columns = lax.axis_size("col")
    full_width = norm1_gain.shape[0] * columns
    query_width = query_weight.shape[1]
    pair_width = key_weight.shape[1]
    hidden_width = gate_weight.shape[1]
    per_column = segments.shape[0] // columns
    seq_length = segments.shape[1]
    local_tokens = per_column * seq_length
    column = lax.axis_index("col")
    first_column = column == 0
    part = hidden_width // 2
    line = LineSum()

    def cut(weight, axis):
        low = lax.slice_in_dim(weight, 0, part, axis=axis)
        high = lax.slice_in_dim(weight, part, 2 * part, axis=axis)
        return jnp.where(first_column, low, high), jnp.where(first_column, high, low)

    even = lax.axis_size("dp") % 2 == 0
    low_plane = (lax.axis_index("dp") & 1) == 0

    def half_of(sent):
        if not even:
            return sent
        half = sent.shape[0] // 2
        return jnp.where(low_plane, sent[:half], sent[half:])

    def share(got):
        return swap(got, "dp", 1) if even else got

    def shared(got, more):
        return pair_up(got, more, low_plane, 0) if even else got

    features = inputs.astype(F32)
    gain_one = norm1_gain.astype(F32)
    gain_two = norm2_gain.astype(F32)
    normed_one, scale_one, hidden_one = norm_forward(features, gain_one, full_width)
    gate, gate_sent = cut(gate_weight, 1)
    up, up_sent = cut(up_weight, 1)
    down, down_sent = cut(down_weight, 0)
    gate_got, down_got, up_got = [
        swap(half_of(part), "col", 1) for part in (gate_sent, down_sent, up_sent)
    ]

    def beside_gather(far):
        nonlocal gate_got
        far, gate_got = order(far, gate_got)
        return far

    one_mine, one_other = gather_row(hidden_one, beside_gather)
    one_other, down_got = order(one_other, down_got)

    qkv_weight = jnp.concatenate([query_weight, key_weight, value_weight], 1)
    local_segments = lax.dynamic_slice_in_dim(segments, column * per_column, per_column, 0)
    positions = jax.vmap(positions_of)(local_segments)
    cosine, sine = rotary_tables(positions)
    starts = (jnp.arange(seq_length, dtype=jnp.int32) - positions)[:, None, :]

    leaving = contract(one_other, qkv_weight).astype(BF)
    leaving, cotangent = order(leaving, cotangent)
    sent = swap(leaving, "col", 1)
    kept = contract(one_mine, qkv_weight)
    along = swap(cotangent, "row", 2)
    kept, sent, along, up_got, cotangent = order(kept, sent, along, up_got, cotangent)
    across = swap(cotangent, "col", 1)
    gate_more, down_more, up_more = share(gate_got), share(down_got), share(up_got)
    attended, queries, kv, log_totals = attention_forward(kept, sent, cosine, sine, starts)
    attended, across, gate_more, down_more = order(attended, across, gate_more, down_more)
    half = cotangent.shape[0] // 2
    corner_second = swap(across[half:], "row", 2)
    cot_near = jnp.concatenate([cotangent, along], 0)
    cot_own = jnp.concatenate([cot_near, swap(cot_near, "row", 1)], 0)
    attended_got = swap(attended, "col", 1)
    attended_got, corner_second, along, up_more = order(attended_got, corner_second, along, up_more)

    corner = [swap(along[:half], "col", 1), corner_second]
    attn_branch = scatter_row((attended, attended_got), lambda rows: contract(rows, out_weight))
    gate_other = shared(gate_got, gate_more)
    down_other = shared(down_got, down_more)
    up_other = shared(up_got, up_more)
    cot_near = jnp.concatenate([across, *corner], 0)
    cot_other = jnp.concatenate([cot_near, swap(cot_near, "row", 1)], 0)
    grad_activated = (
        contract_flipped(cot_own, down) + contract_flipped(cot_other, down_other)
    ).astype(BF)
    attn_branch, grad_activated, gate_other, up_other, cot_own, cot_other = order(
        attn_branch, grad_activated, gate_other, up_other, cot_own, cot_other
    )
    middle = features + attn_branch
    normed_two, scale_two, hidden_two = norm_forward(middle, gain_two, full_width)
    two_own, two_other = gather_plane(hidden_two)
    activated, grad_gate_part, grad_up_part = hidden_part(
        two_own, two_other, gate, gate_other, up, up_other, grad_activated
    )

    done = {}

    def reduce(name, values):
        line.add(values, lambda total: done.__setitem__(name, total))

    down_grad = outer_sum(activated, cot_own)
    down_away = outer_sum(activated, cot_other)
    grad_gate_part, grad_up_part, down_grad, down_away = order(
        grad_gate_part, grad_up_part, down_grad, down_away
    )
    reduce("down_own", down_grad)
    down_away = swap(down_away, "col", 1)
    leaving = back_part(grad_gate_part, grad_up_part, gate, gate_other, up, up_other, 1)
    staying = back_part(grad_gate_part, grad_up_part, gate, gate_other, up, up_other, 0)
    plane = scatter_plane(staying, leaving)
    *plane_leaving, down_away, grad_gate_part, grad_up_part, activated = order(
        *next(plane), down_away, grad_gate_part, grad_up_part, activated
    )
    flight = plane.send(plane_leaving)
    down_away, grad_gate_part, grad_up_part = line.step(down_away, grad_gate_part, grad_up_part)
    reduce("down_other", down_away)
    own = jnp.concatenate(two_own, 0)
    other = jnp.concatenate(two_other, 0)
    gate_grad = outer_sum(grad_gate_part, own)
    gate_other_grad = outer_sum(grad_gate_part, other)
    *flight, gate_grad = line.step(*flight, gate_grad)
    reduce("gate_own", gate_grad)
    grad_hidden_two = plane.send(flight)
    up_grad = outer_sum(grad_up_part, own)
    grad_hidden_two, gate_other_grad, up_grad = order(grad_hidden_two, gate_other_grad, up_grad)
    grad_norm_two, grad_gain_two = norm_backward(
        grad_hidden_two, normed_two, scale_two, gain_two, full_width
    )
    grad_middle = cotangent.astype(F32) + grad_norm_two
    branch_low = grad_middle.astype(BF)
    branch_low, up_grad, gate_other_grad = line.step(branch_low, up_grad, gate_other_grad)
    reduce("up_own", up_grad)
    gate_away = swap(gate_other_grad, "col", 1)
    branch_mine, branch_other = gather_row(branch_low)
    up_other_grad = outer_sum(grad_up_part, other)
    branch_mine, branch_other, gate_away, up_other_grad = line.step(
        branch_mine, branch_other, gate_away, up_other_grad
    )
    reduce("gate_other", gate_away)
    leaving = contract_flipped(branch_other, out_weight).astype(BF)
    grad_sent = swap(leaving, "col", 1)
    grad_kept = contract_flipped(branch_mine, out_weight)
    out_grad = outer_sum(
        jnp.concatenate([attended, attended_got], 0),
        jnp.concatenate([branch_mine, branch_other], 0),
    )
    grad_sent, out_grad, up_other_grad = line.step(grad_sent, out_grad, up_other_grad)
    reduce("out", out_grad)
    up_away = swap(up_other_grad, "col", 1)
    grad_projected = attention_backward(
        grad_kept, grad_sent, queries, kv, log_totals, cosine, sine, starts
    )
    grad_projected, up_away, activated = line.step(grad_projected, up_away, late=(activated,))
    reduce("up_other", up_away)
    projected_got = swap(grad_projected, "col", 1)
    lower = activated.shape[0] // 2
    out_other = contract(activated[:lower], down_other) + swap(
        contract(activated[lower:], down_other).astype(BF), "row", 1
    ).astype(F32)
    out_own = contract(activated[:lower], down) + swap(
        contract(activated[lower:], down).astype(BF), "row", 1
    ).astype(F32)
    projected_got, out_other, out_own, one_mine = line.step(
        projected_got, out_other.astype(BF), late=(out_own, one_mine)
    )
    out_across = swap(out_other, "col", 1)
    qkv_grad = outer_sum(
        jnp.concatenate([one_mine, one_other], 0),
        jnp.concatenate([grad_projected, projected_got], 0),
    )
    reduce("qkv", qkv_grad)
    grad_hidden_one = scatter_row(
        (grad_projected, projected_got), lambda rows: contract_flipped(rows, qkv_weight)
    )
    finished = sorted(done)
    grad_hidden_one, *rest = line.step(grad_hidden_one, *[done[name] for name in finished])
    done.update(zip(finished, rest))
    grad_norm_one, grad_gain_one = norm_backward(
        grad_hidden_one, normed_one, scale_one, gain_one, full_width
    )
    grad_inputs = grad_middle + grad_norm_one
    gain_grads = jnp.stack([grad_gain_one, grad_gain_two])
    for axis in ("row", "dp"):
        size = lax.axis_size(axis)
        if size & (size - 1):
            gain_grads = lax.psum(gain_grads, axis)
            continue
        bit = 1
        while bit < size:
            got = swap(gain_grads, axis, bit)
            if axis == "dp" and bit == 1:
                out_across, got = line.step(out_across, got)
            gain_grads = gain_grads + got
            bit *= 2
    outputs = (middle + scatter_late(out_own, out_across)).astype(BF)
    line.drain()

    def rows_in(name):
        return pair_up(done[name + "_own"], done[name + "_other"], first_column, 0)

    grad_gate = rows_in("gate").T.astype(F32)
    grad_up = rows_in("up").T.astype(F32)
    grad_down = rows_in("down").astype(F32)
    grad_out = done["out"].astype(F32)
    grad_qkv = done["qkv"].astype(F32)
    return (
        outputs,
        grad_inputs,
        gain_grads[0],
        grad_qkv[:, :query_width],
        grad_qkv[:, query_width : query_width + pair_width],
        grad_qkv[:, query_width + pair_width :],
        grad_out,
        gain_grads[1],
        grad_gate,
        grad_up,
        grad_down,
    )


def solution(mesh):
    in_specs = (
        P(("dp", "row"), "col"),
        P("dp", None),
        P("col"),
        P("col", "row"),
        P("col", "row"),
        P("col", "row"),
        P("row", "col"),
        P("col"),
        P("col", "row"),
        P("col", "row"),
        P("row", "col"),
        P(("dp", "row"), "col"),
    )
    out_specs = (
        P(("dp", "row"), "col"),
        P(("dp", "row"), "col"),
        P("col"),
        P("col", "row"),
        P("col", "row"),
        P("col", "row"),
        P("row", "col"),
        P("col"),
        P("col", "row"),
        P("col", "row"),
        P("row", "col"),
    )
    return jax.shard_map(body, mesh=mesh, in_specs=in_specs, out_specs=out_specs, check_vma=False)
```

```python
import jax
import jax.numpy as jnp
from jax import lax
from jax.experimental import pallas as pl
from jax.experimental.pallas import tpu as pltpu
from jax.sharding import PartitionSpec as P

HD = 64
LANES = 128

epsilon = 1e-05
rope_base = 10000.0
BF = jnp.bfloat16
F32 = jnp.float32


def positions_of(segment_row):
    indices = jnp.arange(segment_row.shape[0], dtype=jnp.int32)
    previous = jnp.concatenate([segment_row[:1] - 1, segment_row[:-1]])
    start_index = lax.cummax(jnp.where(segment_row != previous, indices, 0), axis=0)
    return indices - start_index


def rotary_tables(positions):
    frequency = rope_base ** (-jnp.arange(HD // 2).astype(F32) * 2.0 / HD)
    angles = positions.astype(F32)[..., None] * frequency
    cosine = jnp.cos(angles)
    sine = jnp.sin(angles)
    return (
        jnp.concatenate([cosine] * 4, -1),
        jnp.concatenate([-sine, sine, -sine, sine], -1),
    )


def swap(values, axis, bit):
    pairs = [(i, i ^ bit) for i in range(lax.axis_size(axis))]
    return lax.ppermute(values, axis, pairs)


def swap_sum(values):
    return values + swap(values, "col", 1)


def pick(values, index, axis):
    return lax.dynamic_index_in_dim(values, index, axis, keepdims=False)


def pair_up(own, other, first, axis):
    return jnp.concatenate([jnp.where(first, own, other), jnp.where(first, other, own)], axis)


def gather_row(block, between=lambda far: far):
    me = lax.axis_index("row")
    far = swap(block, "row", 2)
    sibling = swap(block, "row", 1)
    far = between(far)
    even = (me & 1) == 0
    near_pair = pair_up(block, sibling, even, 0)
    far_pair = pair_up(far, swap(far, "row", 1), even, 0)
    mine = (me >> 1) == lax.axis_index("col")
    return jnp.where(mine, near_pair, far_pair), jnp.where(mine, far_pair, near_pair)


def scatter_row(sequences, product):
    me = lax.axis_index("row")
    parity = me & 1
    block = sequences[0].shape[0] // 2

    def rows(index):
        parts = [lax.dynamic_slice_in_dim(rows, index * block, block, 0) for rows in sequences]
        return jnp.concatenate(parts, 0)

    sent = product(rows(1 - parity)).astype(BF)
    arrived = swap(sent, "row", 1)
    kept = product(rows(parity))
    both = (kept + arrived.astype(F32)).reshape(2, block, -1)
    where = (me >> 1) ^ lax.axis_index("col")
    return pick(both, where, 0) + swap(pick(both, 1 - where, 0).astype(BF), "row", 2).astype(F32)


def gather_plane(block):
    half = block.shape[0] // 2
    across, along = swap(block, "col", 1), swap(block, "row", 2)
    corner = swap(along[:half], "col", 1), swap(across[half:], "row", 2)
    own = jnp.concatenate([block, along], 0)
    other = jnp.concatenate([across, *corner], 0)
    return (own, swap(own, "row", 1)), (other, swap(other, "row", 1))


def scatter_plane(kept, sent):
    arrived = [swap(values, "row", 1) for values in sent]
    own, other = [
        (values.astype(F32) + more.astype(F32)).reshape(2, -1, values.shape[1])
        for values, more in zip(kept, arrived)
    ]
    half = own.shape[1] // 2
    first_own, first_other = own[:, :half], other[:, :half].astype(BF)
    second_own, second_other = own[0, half:], other[0, half:]
    leaving = first_other, own[1, half:].astype(BF), other[1, half:].astype(BF)
    leaving = yield leaving
    got = swap(leaving[0], "col", 1), swap(leaving[1], "row", 2), swap(leaving[2], "row", 2)
    first_got, second_got_own, second_got_other = yield got
    first_sum = first_own + first_got.astype(F32)
    second_mine = second_own + second_got_own.astype(F32)
    second_theirs = (second_other + second_got_other.astype(F32)).astype(BF)
    first_sum = first_sum[0] + swap(first_sum[1].astype(BF), "row", 2).astype(F32)
    second_sum = second_mine + swap(second_theirs, "col", 1).astype(F32)
    yield jnp.concatenate([first_sum, second_sum], 0)


def scatter_late(own, across):
    both = (own + across.astype(F32)).reshape(2, -1, own.shape[1])
    return both[0] + swap(both[1].astype(BF), "row", 2).astype(F32)


def order(*values):
    return lax.optimization_barrier(values)


class LineSum:
    stages = ([(0, 1), (3, 2)], [(1, 2), (2, 1)], [(1, 0), (2, 3)])

    def __init__(self):
        self.line = lax.axis_size("dp") == 4
        self.flight = []

    def add(self, values, finish):
        if self.line:
            self.flight.append([1, values, lax.ppermute(values, "dp", self.stages[0]), finish])
        else:
            mine = lax.psum_scatter(values, "dp", scatter_dimension=0, tiled=True)
            finish(lax.all_gather(mine, "dp", axis=0, tiled=True))

    def step(self, *anchors, late=()):
        moving = list(self.flight)
        results = order(*anchors, *late, *[item[2] for item in moving])
        kept, late, got = (
            results[: len(anchors)],
            results[len(anchors) : len(anchors) + len(late)],
            results[len(anchors) + len(late) :],
        )
        place = lax.axis_index("dp")
        going = []
        for item, arrived in zip(moving, got):
            stage, values, _, finish = item
            if stage == 3:
                finish(jnp.where((place == 0) | (place == 3), arrived, values))
                self.flight.remove(item)
                continue
            item[1] = (values.astype(F32) + arrived.astype(F32)).astype(values.dtype)
            going.append(item)
        if late:
            results = order(*late, *[item[1] for item in going])
            late = results[: len(late)]
            for item, values in zip(going, results[len(late) :]):
                item[1] = values
        for item in going:
            item[2] = lax.ppermute(item[1], "dp", self.stages[item[0]])
            item[0] += 1
        return (*kept, *late)

    def drain(self):
        while self.flight:
            self.step()


def norm_forward(values, gain, full_width):
    squares = swap_sum(jnp.sum(values * values, -1, keepdims=True))
    scale = lax.rsqrt(squares / full_width + epsilon)
    normed = values * scale
    return (normed, scale, (normed * gain).astype(BF))


def norm_backward(grad_hidden, normed, scale, gain, full_width):
    grad_normed = grad_hidden * gain
    inner_sum = swap_sum(jnp.sum(grad_normed * normed, -1, keepdims=True))
    return (
        scale * (grad_normed - normed * inner_sum / full_width),
        jnp.sum(grad_hidden * normed, 0),
    )


def contract(leading, weight):
    return jnp.dot(leading, weight, preferred_element_type=F32)


def contract_flipped(leading, weight):
    return lax.dot_general(
        leading, weight, (((1,), (1,)), ((), ())), preferred_element_type=F32
    )


def outer_sum(leading, trailing):
    return lax.dot_general(
        leading, trailing, (((0,), (0,)), ((), ())), preferred_element_type=F32
    ).astype(BF)


ROWS = 256
PAIR = 2 * HD


def dot_nt(leading, trailing):
    return lax.dot_general(leading, trailing, (((1,), (1,)), ((), ())), preferred_element_type=F32)


def dot_nn(leading, trailing):
    return jnp.dot(leading, trailing, preferred_element_type=F32)


def turn(vectors, cosine, sine, lane):
    ahead = pltpu.roll(vectors, PAIR - HD // 2, 1)
    behind = pltpu.roll(vectors, HD // 2, 1)
    return vectors * cosine + jnp.where(lane % HD < HD // 2, ahead, behind) * sine


def fill_bias(starts_ref, bias):
    length = bias.shape[0]
    for base in range(0, length, ROWS):
        key = lax.broadcasted_iota(jnp.int32, (ROWS, length), 0) + base
        query = lax.broadcasted_iota(jnp.int32, (ROWS, length), 1)
        allowed = (key <= query) & (key >= starts_ref[0])
        bias[base : base + ROWS, :] = jnp.where(allowed, 0.0, -1e30)


def split_heads(values, lane):
    low = jnp.where(lane < HD, values, 0.0)
    return low, pltpu.roll(low, HD, 1)


def forward_kernel(
    kept_ref, sent_ref, kept_kv_ref, sent_kv_ref, cos_ref, sin_ref, starts_ref, *rest, anchors
):
    att_ref, q_ref, kv_ref, lse_ref, keys, values_t, bias = rest[anchors:]
    length = kept_ref.shape[0]
    lane = lax.broadcasted_iota(jnp.int32, (length, PAIR), 1)

    @pl.when(pl.program_id(1) == 0)
    def _():
        joined = kept_kv_ref[...].astype(F32) + sent_kv_ref[...].astype(F32)
        turned = turn(joined, cos_ref[0], sin_ref[0], lane)
        low = jnp.where(lane < HD, turned, joined).astype(BF)
        kv_ref[...] = low
        wide = low.astype(F32)
        key_a, key_b = split_heads(wide, lane)
        keys[0] = key_a.astype(BF)
        keys[1] = key_b.astype(BF)
        value_a, value_b = split_heads(pltpu.roll(wide, HD, 1), lane)
        values_t[0] = value_a.T.astype(BF)
        values_t[1] = value_b.T.astype(BF)
        fill_bias(starts_ref, bias)

    joined = kept_ref[...].astype(F32) + sent_ref[...].astype(F32)
    queries = turn(joined, cos_ref[0], sin_ref[0], lane).astype(BF)
    q_ref[...] = queries
    queries = queries * jnp.asarray(HD**-0.5, BF)
    for base in range(0, length, ROWS):
        block = queries[base : base + ROWS]
        count = base + ROWS
        mixed = jnp.zeros((PAIR, ROWS), F32)
        for head in range(2):
            scores = dot_nt(keys[head, :count], block) + bias[:count, base:count]
            highest = jnp.max(scores, 0, keepdims=True)
            weights = jnp.exp(scores - highest)
            total = jnp.sum(weights, 0, keepdims=True)
            part = dot_nn(values_t[head, :, :count], weights.astype(BF))
            mixed = mixed + part / total
            lse_ref[0, head : head + 1, base:count] = highest + jnp.log(total)
        att_ref[base:count, :] = mixed.T.astype(BF)


def backward_kernel(
    kept_ref, sent_ref, q_ref, kv_ref, lse_ref, cos_ref, sin_ref, starts_ref, *rest, anchors
):
    grad_ref, keys, keys_t, values, bias, grad_keys, grad_values = rest[anchors:]
    length = kv_ref.shape[0]
    lane = lax.broadcasted_iota(jnp.int32, (length, PAIR), 1)
    step = pl.program_id(1)
    last = pl.num_programs(1) - 1

    @pl.when(step == 0)
    def _():
        wide = kv_ref[...].astype(F32)
        for head, part in enumerate(split_heads(wide, lane)):
            keys[head] = part.astype(BF)
            keys_t[head] = part.T.astype(BF)
        for head, part in enumerate(split_heads(pltpu.roll(wide, HD, 1), lane)):
            values[head] = part.astype(BF)
        fill_bias(starts_ref, bias)
        grad_keys[...] = jnp.zeros_like(grad_keys)
        grad_values[...] = jnp.zeros_like(grad_values)

    @pl.when(step < last)
    def _():
        given = (kept_ref[...].astype(F32) + sent_ref[...].astype(F32)).astype(BF)
        queries = q_ref[...] * jnp.asarray(HD**-0.5, BF)
        zero = jnp.zeros_like(given)
        for base in range(0, length, ROWS):
            count = base + ROWS
            block = queries[base:count]
            gave = given[base:count]
            side = lane[base:count] < HD
            grad_t = jnp.zeros((PAIR, ROWS), F32)
            for head in range(2):
                mine = side if head == 0 else jnp.logical_not(side)
                block_mine = jnp.where(mine, block, zero[:ROWS])
                gave_mine = jnp.where(mine, gave, zero[:ROWS])
                scores = dot_nt(keys[head, :count], block) + bias[:count, base:count]
                weights = jnp.exp(scores - lse_ref[0, head : head + 1, base:count])
                grad_weights = dot_nt(values[head, :count], gave)
                product = weights * grad_weights
                inner = jnp.sum(product, 0, keepdims=True)
                grad_scores = (product - weights * inner).astype(BF)
                grad_values[:count] += dot_nn(weights.astype(BF), gave_mine)
                grad_keys[:count] += dot_nn(grad_scores, block_mine)
                grad_t = grad_t + dot_nn(keys_t[head, :, :count], grad_scores)
            grad = grad_t.T * HD**-0.5
            grad_ref[base:count, :] = turn(
                grad, cos_ref[0, base:count], -sin_ref[0, base:count], lane[base:count]
            ).astype(BF)

    @pl.when(step == last)
    def _():
        key_sum = grad_keys[...] + pltpu.roll(grad_keys[...], HD, 1)
        value_sum = grad_values[...] + pltpu.roll(grad_values[...], HD, 1)
        turned = turn(key_sum, cos_ref[0], -sin_ref[0], lane)
        grad_ref[...] = jnp.where(lane < HD, turned, value_sum).astype(BF)


VMEM = 48 * 1024 * 1024


def hidden_kernel(
    own_ref, own_sibling_ref, other_ref, other_sibling_ref,
    gate_ref, gate_other_ref, up_ref, up_other_ref, given_ref,
    act_ref, grad_gate_ref, grad_up_ref,
):
    def tile(own_ref, other_ref):
        own, other = own_ref[...], other_ref[...]
        gate = dot_nn(own, gate_ref[...]) + dot_nn(other, gate_other_ref[...])
        up = dot_nn(own, up_ref[...]) + dot_nn(other, up_other_ref[...])
        given = given_ref[...].astype(F32)
        bent = 1.0 / (1.0 + jnp.exp(-gate))
        silu = gate * bent
        act_ref[...] = (silu * up).astype(BF)
        grad_gate_ref[...] = (given * up * bent * (1.0 + gate * (1.0 - bent))).astype(BF)
        grad_up_ref[...] = (given * silu).astype(BF)

    near = pl.program_id(0) < pl.num_programs(0) // 2

    @pl.when(near)
    def _():
        tile(own_ref, other_ref)

    @pl.when(jnp.logical_not(near))
    def _():
        tile(own_sibling_ref, other_sibling_ref)


def hidden_part(own, other, gate, gate_other, up, up_other, given):
    tokens, hidden = given.shape
    width = gate.shape[0]
    half = tokens // ROWS // 2
    rows = pl.BlockSpec((ROWS, hidden), lambda i: (i, 0))
    near = pl.BlockSpec((ROWS, width), lambda i: (jnp.minimum(i, half - 1), 0))
    sibling = pl.BlockSpec((ROWS, width), lambda i: (jnp.maximum(i - half, 0), 0))
    whole = pl.BlockSpec((width, hidden), lambda i: (0, 0))
    return pl.pallas_call(
        hidden_kernel,
        grid=(2 * half,),
        in_specs=[near, sibling, near, sibling, whole, whole, whole, whole, rows],
        out_specs=[rows] * 3,
        out_shape=[jax.ShapeDtypeStruct((tokens, hidden), BF)] * 3,
        compiler_params=pltpu.CompilerParams(vmem_limit_bytes=VMEM),
        cost_estimate=pl.CostEstimate(
            flops=8 * tokens * width * hidden, bytes_accessed=24 * 2**20, transcendentals=0
        ),
        name="hidden_part",
    )(*own, *other, gate, gate_other, up, up_other, given)


def back_kernel(grad_gate_ref, grad_up_ref, gate_ref, gate_other_ref, up_ref, up_other_ref, own_ref, other_ref):
    grad_gate, grad_up = grad_gate_ref[...], grad_up_ref[...]
    own_ref[...] = (dot_nt(grad_gate, gate_ref[...]) + dot_nt(grad_up, up_ref[...])).astype(BF)
    other_ref[...] = (
        dot_nt(grad_gate, gate_other_ref[...]) + dot_nt(grad_up, up_other_ref[...])
    ).astype(BF)


def back_part(grad_gate, grad_up, gate, gate_other, up, up_other, half):
    hidden = grad_gate.shape[1]
    tokens = grad_gate.shape[0] // 2
    width = gate.shape[0]
    steps = tokens // ROWS
    rows = pl.BlockSpec((ROWS, hidden), lambda i: (i + half * steps, 0))
    whole = pl.BlockSpec((width, hidden), lambda i: (0, 0))
    return pl.pallas_call(
        back_kernel,
        grid=(steps,),
        in_specs=[rows, rows, whole, whole, whole, whole],
        out_specs=[pl.BlockSpec((ROWS, width), lambda i: (i, 0))] * 2,
        out_shape=[jax.ShapeDtypeStruct((tokens, width), BF)] * 2,
        compiler_params=pltpu.CompilerParams(vmem_limit_bytes=VMEM),
        cost_estimate=pl.CostEstimate(
            flops=8 * tokens * width * hidden, bytes_accessed=12 * 2**20, transcendentals=0
        ),
        name="back_part",
    )(grad_gate, grad_up, gate, gate_other, up, up_other)


def attention_forward(kept, sent, cosine, sine, starts, anchors=()):
    sequences, _, length = starts.shape
    pairs = kept.shape[1] // PAIR - 1
    here = lambda s, i: (s, i)
    kv_at = lambda s, i: (s, pairs)
    table = pl.BlockSpec((1, length, PAIR), lambda s, i: (s, 0, 0))
    return pl.pallas_call(
        lambda *refs: forward_kernel(*refs, anchors=len(anchors)),
        grid=(sequences, pairs),
        in_specs=[
            pl.BlockSpec((length, PAIR), here),
            pl.BlockSpec((length, PAIR), here),
            pl.BlockSpec((length, PAIR), kv_at),
            pl.BlockSpec((length, PAIR), kv_at),
            table,
            table,
            pl.BlockSpec((1, 1, length), lambda s, i: (s, 0, 0)),
        ]
        + [pl.BlockSpec(memory_space=pl.ANY)] * len(anchors),
        out_specs=[
            pl.BlockSpec((length, PAIR), here),
            pl.BlockSpec((length, PAIR), here),
            pl.BlockSpec((length, PAIR), lambda s, i: (s, 0)),
            pl.BlockSpec((1, 2, length), lambda s, i: (s * pairs + i, 0, 0)),
        ],
        out_shape=[
            jax.ShapeDtypeStruct((sequences * length, pairs * PAIR), BF),
            jax.ShapeDtypeStruct((sequences * length, pairs * PAIR), BF),
            jax.ShapeDtypeStruct((sequences * length, PAIR), BF),
            jax.ShapeDtypeStruct((sequences * pairs, 2, length), F32),
        ],
        scratch_shapes=[
            pltpu.VMEM((2, length, PAIR), BF),
            pltpu.VMEM((2, PAIR, length), BF),
            pltpu.VMEM((length, length), F32),
        ],
        compiler_params=pltpu.CompilerParams(vmem_limit_bytes=VMEM),
        cost_estimate=pl.CostEstimate(
            flops=20 * 10**9, bytes_accessed=8 * 2**20, transcendentals=0
        ),
        name="attention_forward",
    )(kept, sent, kept, sent, cosine, sine, starts, *anchors)


def attention_backward(kept, sent, queries, kv, log_totals, cosine, sine, starts, anchors=()):
    sequences, _, length = starts.shape
    pairs = queries.shape[1] // PAIR
    here = lambda s, i: (s, jnp.minimum(i, pairs - 1))
    table = pl.BlockSpec((1, length, PAIR), lambda s, i: (s, 0, 0))
    return pl.pallas_call(
        lambda *refs: backward_kernel(*refs, anchors=len(anchors)),
        grid=(sequences, pairs + 1),
        in_specs=[
            pl.BlockSpec((length, PAIR), here),
            pl.BlockSpec((length, PAIR), here),
            pl.BlockSpec((length, PAIR), here),
            pl.BlockSpec((length, PAIR), lambda s, i: (s, 0)),
            pl.BlockSpec(
                (1, 2, length), lambda s, i: (s * pairs + jnp.minimum(i, pairs - 1), 0, 0)
            ),
            table,
            table,
            pl.BlockSpec((1, 1, length), lambda s, i: (s, 0, 0)),
        ]
        + [pl.BlockSpec(memory_space=pl.ANY)] * len(anchors),
        out_specs=pl.BlockSpec((length, PAIR), lambda s, i: (s, i)),
        out_shape=jax.ShapeDtypeStruct((sequences * length, (pairs + 1) * PAIR), BF),
        scratch_shapes=[
            pltpu.VMEM((2, length, PAIR), BF),
            pltpu.VMEM((2, PAIR, length), BF),
            pltpu.VMEM((2, length, PAIR), BF),
            pltpu.VMEM((length, length), F32),
            pltpu.VMEM((length, PAIR), F32),
            pltpu.VMEM((length, PAIR), F32),
        ],
        compiler_params=pltpu.CompilerParams(vmem_limit_bytes=VMEM),
        cost_estimate=pl.CostEstimate(
            flops=40 * 10**9, bytes_accessed=8 * 2**20, transcendentals=0
        ),
        name="attention_backward",
    )(kept, sent, queries, kv, log_totals, cosine, sine, starts, *anchors)


def body(
    inputs,
    segments,
    norm1_gain,
    query_weight,
    key_weight,
    value_weight,
    out_weight,
    norm2_gain,
    gate_weight,
    up_weight,
    down_weight,
    cotangent,
):
    columns = lax.axis_size("col")
    full_width = norm1_gain.shape[0] * columns
    query_width = query_weight.shape[1]
    pair_width = key_weight.shape[1]
    hidden_width = gate_weight.shape[1]
    per_column = segments.shape[0] // columns
    seq_length = segments.shape[1]
    local_tokens = per_column * seq_length
    column = lax.axis_index("col")
    first_column = column == 0
    part = hidden_width // 2
    line = LineSum()

    def cut(weight, axis):
        low = lax.slice_in_dim(weight, 0, part, axis=axis)
        high = lax.slice_in_dim(weight, part, 2 * part, axis=axis)
        return jnp.where(first_column, low, high), jnp.where(first_column, high, low)

    even = lax.axis_size("dp") % 2 == 0
    low_plane = (lax.axis_index("dp") & 1) == 0

    def half_of(sent):
        if not even:
            return sent
        half = sent.shape[0] // 2
        return jnp.where(low_plane, sent[:half], sent[half:])

    def share(got):
        return swap(got, "dp", 1) if even else got

    def shared(got, more):
        return pair_up(got, more, low_plane, 0) if even else got

    features = inputs.astype(F32)
    gain_one = norm1_gain.astype(F32)
    gain_two = norm2_gain.astype(F32)
    normed_one, scale_one, hidden_one = norm_forward(features, gain_one, full_width)
    gate, gate_sent = cut(gate_weight, 1)
    up, up_sent = cut(up_weight, 1)
    down, down_sent = cut(down_weight, 0)
    gate_got, down_got, up_got = [
        swap(half_of(part), "col", 1) for part in (gate_sent, down_sent, up_sent)
    ]

    def beside_gather(far):
        nonlocal gate_got
        far, gate_got = order(far, gate_got)
        return far

    one_mine, one_other = gather_row(hidden_one, beside_gather)
    one_other, down_got = order(one_other, down_got)

    qkv_weight = jnp.concatenate([query_weight, key_weight, value_weight], 1)
    local_segments = lax.dynamic_slice_in_dim(segments, column * per_column, per_column, 0)
    positions = jax.vmap(positions_of)(local_segments)
    cosine, sine = rotary_tables(positions)
    starts = (jnp.arange(seq_length, dtype=jnp.int32) - positions)[:, None, :]

    leaving = contract(one_other, qkv_weight).astype(BF)
    leaving, cotangent = order(leaving, cotangent)
    sent = swap(leaving, "col", 1)
    kept = contract(one_mine, qkv_weight)
    along = swap(cotangent, "row", 2)
    kept, sent, along, up_got, cotangent = order(kept, sent, along, up_got, cotangent)
    across = swap(cotangent, "col", 1)
    gate_more, down_more, up_more = share(gate_got), share(down_got), share(up_got)
    attended, queries, kv, log_totals = attention_forward(kept, sent, cosine, sine, starts)
    attended, across, gate_more, down_more = order(attended, across, gate_more, down_more)
    half = cotangent.shape[0] // 2
    corner_second = swap(across[half:], "row", 2)
    cot_near = jnp.concatenate([cotangent, along], 0)
    cot_own = jnp.concatenate([cot_near, swap(cot_near, "row", 1)], 0)
    attended_got = swap(attended, "col", 1)
    attended_got, corner_second, along, up_more = order(attended_got, corner_second, along, up_more)

    corner = [swap(along[:half], "col", 1), corner_second]
    attn_branch = scatter_row((attended, attended_got), lambda rows: contract(rows, out_weight))
    gate_other = shared(gate_got, gate_more)
    down_other = shared(down_got, down_more)
    up_other = shared(up_got, up_more)
    cot_near = jnp.concatenate([across, *corner], 0)
    cot_other = jnp.concatenate([cot_near, swap(cot_near, "row", 1)], 0)
    grad_activated = (
        contract_flipped(cot_own, down) + contract_flipped(cot_other, down_other)
    ).astype(BF)
    attn_branch, grad_activated, gate_other, up_other, cot_own, cot_other = order(
        attn_branch, grad_activated, gate_other, up_other, cot_own, cot_other
    )
    middle = features + attn_branch
    normed_two, scale_two, hidden_two = norm_forward(middle, gain_two, full_width)
    two_own, two_other = gather_plane(hidden_two)
    activated, grad_gate_part, grad_up_part = hidden_part(
        two_own, two_other, gate, gate_other, up, up_other, grad_activated
    )

    done = {}

    def reduce(name, values):
        line.add(values, lambda total: done.__setitem__(name, total))

    down_grad = outer_sum(activated, cot_own)
    down_away = outer_sum(activated, cot_other)
    grad_gate_part, grad_up_part, down_grad, down_away = order(
        grad_gate_part, grad_up_part, down_grad, down_away
    )
    reduce("down_own", down_grad)
    down_away = swap(down_away, "col", 1)
    leaving = back_part(grad_gate_part, grad_up_part, gate, gate_other, up, up_other, 1)
    staying = back_part(grad_gate_part, grad_up_part, gate, gate_other, up, up_other, 0)
    plane = scatter_plane(staying, leaving)
    *plane_leaving, down_away, grad_gate_part, grad_up_part, activated = order(
        *next(plane), down_away, grad_gate_part, grad_up_part, activated
    )
    flight = plane.send(plane_leaving)
    down_away, grad_gate_part, grad_up_part = line.step(down_away, grad_gate_part, grad_up_part)
    reduce("down_other", down_away)
    own = jnp.concatenate(two_own, 0)
    other = jnp.concatenate(two_other, 0)
    gate_grad = outer_sum(grad_gate_part, own)
    gate_other_grad = outer_sum(grad_gate_part, other)
    *flight, gate_grad = line.step(*flight, gate_grad)
    reduce("gate_own", gate_grad)
    grad_hidden_two = plane.send(flight)
    up_grad = outer_sum(grad_up_part, own)
    grad_hidden_two, gate_other_grad, up_grad = order(grad_hidden_two, gate_other_grad, up_grad)
    grad_norm_two, grad_gain_two = norm_backward(
        grad_hidden_two, normed_two, scale_two, gain_two, full_width
    )
    grad_middle = cotangent.astype(F32) + grad_norm_two
    branch_low = grad_middle.astype(BF)
    up_grad, gate_other_grad = line.step(up_grad, gate_other_grad)
    reduce("up_own", up_grad)
    gate_away = swap(gate_other_grad, "col", 1)
    branch_mine, branch_other = gather_row(branch_low)
    up_other_grad = outer_sum(grad_up_part, other)
    branch_mine, branch_other, gate_away, up_other_grad = line.step(
        branch_mine, branch_other, gate_away, up_other_grad
    )
    reduce("gate_other", gate_away)
    leaving = contract_flipped(branch_other, out_weight).astype(BF)
    grad_sent = swap(leaving, "col", 1)
    grad_kept = contract_flipped(branch_mine, out_weight)
    out_grad = outer_sum(
        jnp.concatenate([attended, attended_got], 0),
        jnp.concatenate([branch_mine, branch_other], 0),
    )
    grad_sent, out_grad, up_other_grad = line.step(grad_sent, out_grad, up_other_grad)
    reduce("out", out_grad)
    up_away = swap(up_other_grad, "col", 1)
    grad_projected = attention_backward(
        grad_kept, grad_sent, queries, kv, log_totals, cosine, sine, starts
    )
    grad_projected, up_away, activated = line.step(grad_projected, up_away, late=(activated,))
    reduce("up_other", up_away)
    projected_got = swap(grad_projected, "col", 1)
    lower = activated.shape[0] // 2
    out_other = contract(activated[:lower], down_other) + swap(
        contract(activated[lower:], down_other).astype(BF), "row", 1
    ).astype(F32)
    out_own = contract(activated[:lower], down) + swap(
        contract(activated[lower:], down).astype(BF), "row", 1
    ).astype(F32)
    projected_got, out_other, out_own, one_mine = line.step(
        projected_got, out_other.astype(BF), late=(out_own, one_mine)
    )
    out_across = swap(out_other, "col", 1)
    qkv_grad = outer_sum(
        jnp.concatenate([one_mine, one_other], 0),
        jnp.concatenate([grad_projected, projected_got], 0),
    )
    reduce("qkv", qkv_grad)
    grad_hidden_one = scatter_row(
        (grad_projected, projected_got), lambda rows: contract_flipped(rows, qkv_weight)
    )
    finished = sorted(done)
    grad_hidden_one, *rest = line.step(grad_hidden_one, *[done[name] for name in finished])
    done.update(zip(finished, rest))
    grad_norm_one, grad_gain_one = norm_backward(
        grad_hidden_one, normed_one, scale_one, gain_one, full_width
    )
    grad_inputs = grad_middle + grad_norm_one
    gain_grads = jnp.stack([grad_gain_one, grad_gain_two])
    for axis in ("row", "dp"):
        size = lax.axis_size(axis)
        if size & (size - 1):
            gain_grads = lax.psum(gain_grads, axis)
            continue
        bit = 1
        while bit < size:
            got = swap(gain_grads, axis, bit)
            if axis == "dp" and bit == 1:
                out_across, got = line.step(out_across, got)
            gain_grads = gain_grads + got
            bit *= 2
    outputs = (middle + scatter_late(out_own, out_across)).astype(BF)
    line.drain()

    def rows_in(name):
        return pair_up(done[name + "_own"], done[name + "_other"], first_column, 0)

    grad_gate = rows_in("gate").T.astype(F32)
    grad_up = rows_in("up").T.astype(F32)
    grad_down = rows_in("down").astype(F32)
    grad_out = done["out"].astype(F32)
    grad_qkv = done["qkv"].astype(F32)
    return (
        outputs,
        grad_inputs,
        gain_grads[0],
        grad_qkv[:, :query_width],
        grad_qkv[:, query_width : query_width + pair_width],
        grad_qkv[:, query_width + pair_width :],
        grad_out,
        gain_grads[1],
        grad_gate,
        grad_up,
        grad_down,
    )


def solution(mesh):
    in_specs = (
        P(("dp", "row"), "col"),
        P("dp", None),
        P("col"),
        P("col", "row"),
        P("col", "row"),
        P("col", "row"),
        P("row", "col"),
        P("col"),
        P("col", "row"),
        P("col", "row"),
        P("row", "col"),
        P(("dp", "row"), "col"),
    )
    out_specs = (
        P(("dp", "row"), "col"),
        P(("dp", "row"), "col"),
        P("col"),
        P("col", "row"),
        P("col", "row"),
        P("col", "row"),
        P("row", "col"),
        P("col"),
        P("col", "row"),
        P("col", "row"),
        P("row", "col"),
    )
    return jax.shard_map(body, mesh=mesh, in_specs=in_specs, out_specs=out_specs, check_vma=False)
```
